256 devices in a mesh: kv: 64 (over z, y, core), head: 4 (over x).
Axes of the slice: x: 4, y: 4, z: 8, core: 2. Of those that a mesh axis runs over, the one named last changes fastest.
Arguments:
- queries: bfloat16 [64, 128, 576], P('kv', 'head'), may hold values from -512 to 512
- prompt_cache: bfloat16 [2, 65536, 576], P(None, 'kv'), may hold values from -6 to 6
- suffix_cache: bfloat16 [64, 2048, 576], P(None, 'kv'), may hold values from -6 to 6
- prompt_ids: int32 [64], replicated, may hold values from 0 to 1, as said below
- suffix_len: int32 [64], replicated, may hold values from 128 to 2048, as said below
- w_uv: bfloat16 [128, 512, 128], P('head'), may hold values from -2.5 to 2.5
- w_out: bfloat16 [16384, 7168], P('head', 'kv'), may hold values from -0.046875 to 0.046875
Outputs:
- mixed: bfloat16 [64, 7168], P(None, ('kv', 'head'))
The draws below stay inside these ranges and needn't reach their ends.
Inputs may be any that keep to these rules, and one draw needn't show every extreme that they name: `prompt_ids`: each prompt id is used by exactly 32 rows. `suffix_len`: every length is a whole number of blocks of 128; some row reaches 2048.
All inputs are finite; a program needn't handle non-finite values.
Results may differ from the reference program's by a relative error of at most 0.01.
Values may be sent and summed in bfloat16 or wider, within the bound.
No kernel may reach another device: no remote copies, remote signals or barrier semaphores. Data moves between devices by JAX's collectives and lax.ppermute only.
A program may use at most 128 MiB of HBM per device.

```python
import jax
import jax.numpy as jnp
from jax import lax

D = 7168
HEADS = 128
LAT = 512
ROPE = 64
NOPE = 128
VH = 128
PROMPTS = 2
SAMPLES = 32
BLOCK = 128
ROWS = 64
PLEN = 65536
SUF_MAX = 2048


def prompt_rows(key):
    labels = jnp.repeat(jnp.arange(PROMPTS, dtype=jnp.int32), SAMPLES)
    return jax.random.permutation(jax.random.fold_in(key, 11), labels)


def base_cache(key):
    return jnp.clip(jax.random.normal(jax.random.fold_in(key, 5), (PROMPTS, PLEN, LAT + ROPE), jnp.float32), -6.0, 6.0)


def draw_prompt_ids(key, part):
    return prompt_rows(key).astype(jnp.int32)


def draw_suffix_len(key, part):
    own = jax.random.fold_in(key, 3)
    blocks_max = SUF_MAX // BLOCK
    blocks = jax.random.randint(jax.random.fold_in(own, 1), (ROWS,), 1, blocks_max + 1)
    chosen_row = jax.random.randint(jax.random.fold_in(own, 2), (), 0, ROWS)
    blocks = blocks.at[chosen_row].set(blocks_max)
    return (blocks * BLOCK).astype(jnp.int32)


def draw_prompt_cache(key, part):
    cache = base_cache(key)
    return cache.astype(jnp.bfloat16)


def draw_queries(key, part):
    own = jax.random.fold_in(key, 9)
    values = 1.5 * jnp.clip(jax.random.normal(own, (ROWS, HEADS, LAT + ROPE), jnp.float32), -6.0, 6.0)
    return values.astype(jnp.bfloat16)


def shard_levels(rng, extent, shards, smallest, largest):
    def one(dim, parts):
        heights = jax.random.uniform(jax.random.fold_in(jax.random.fold_in(rng, 6), dim), (parts,), jnp.float32, smallest / len(shards), largest / len(shards))
        return jnp.repeat(jnp.exp(heights), extent[dim] // parts).reshape((-1,) + (1,) * (len(extent) - dim - 1))

    loudness = one(*shards[0])
    for cut in shards[1:]:
        loudness = loudness * one(*cut)
    return loudness


def gaussian(own_key, dims, deviation, reach, cuts=(), kind=jnp.bfloat16):
    values = jax.random.normal(own_key, dims, jnp.float32) * deviation
    if len(cuts) > 0:
        values = shard_levels(own_key, dims, cuts, -0.22, 0.18) * values
    return jnp.clip(values, min=-reach, max=reach).astype(kind)


def setup_inputs(seed: int = 0) -> dict:
    seeds = jax.random.split(jax.random.key(seed), 8)
    queries = draw_queries(jax.random.fold_in(seeds[7], 71), 0)
    prompt_cache = draw_prompt_cache(jax.random.fold_in(seeds[7], 71), 0)
    suffix_cache = gaussian(seeds[2], (ROWS, SUF_MAX, LAT + ROPE), 1.0, 6.0, ((1, 64),))
    prompt_ids = draw_prompt_ids(jax.random.fold_in(seeds[7], 71), 0)
    suffix_len = draw_suffix_len(jax.random.fold_in(seeds[7], 71), 0)
    w_uv = gaussian(seeds[5], (HEADS, LAT, VH), 0.35, 2.5, ((0, 4),))
    w_out = gaussian(seeds[6], (HEADS * VH, D), (HEADS * VH) ** -0.5, 0.046875, ((0, 4), (1, 64)))
    return dict(queries=queries, prompt_cache=prompt_cache, suffix_cache=suffix_cache, prompt_ids=prompt_ids, suffix_len=suffix_len, w_uv=w_uv, w_out=w_out)


def reference(queries, prompt_cache, suffix_cache, prompt_ids, suffix_len, w_uv, w_out):
    score_scale = (NOPE + ROPE) ** -0.5
    members = ROWS // PROMPTS
    ordering = jnp.argsort(prompt_ids, stable=True).astype(jnp.int32)
    inverse = jnp.argsort(ordering, stable=True).astype(jnp.int32)
    sorted_queries = jnp.transpose(queries[ordering], (1, 0, 2))
    sorted_suffix = suffix_cache[ordering].astype(jnp.float32)
    sorted_len = suffix_len[ordering]
    position = jnp.arange(SUF_MAX, dtype=jnp.int32)
    allowed = position[None, :] < sorted_len[:, None]
    latent_prompt = prompt_cache[:, :, :LAT]

    def one_head(operands):
        query_head, uv_head = operands
        prefix_scores = jnp.concatenate([jnp.dot(query_head[k * members:(k + 1) * members], prompt_cache[k].T, preferred_element_type=jnp.float32) for k in range(PROMPTS)], axis=0) * score_scale
        suffix_scores = jnp.einsum('re,rte->rt', query_head.astype(jnp.float32), sorted_suffix) * score_scale
        suffix_scores = jnp.where(allowed, suffix_scores, -jnp.inf)
        maximum_score = jnp.maximum(prefix_scores.max(-1), suffix_scores.max(-1))
        prefix_weights = jnp.exp(prefix_scores - maximum_score[:, None])
        suffix_weights = jnp.exp(suffix_scores - maximum_score[:, None])
        denominator = prefix_weights.sum(-1) + suffix_weights.sum(-1)
        prefix_rounded = prefix_weights.astype(jnp.bfloat16)
        suffix_rounded = lax.optimization_barrier(suffix_weights.astype(jnp.bfloat16)).astype(jnp.float32)
        attended = jnp.concatenate([jnp.dot(prefix_rounded[k * members:(k + 1) * members], latent_prompt[k], preferred_element_type=jnp.float32) for k in range(PROMPTS)], axis=0)
        attended = attended + jnp.einsum('rt,rtl->rl', suffix_rounded, sorted_suffix[:, :, :LAT])
        attended = attended / denominator[:, None]
        return jnp.dot(attended, uv_head.astype(jnp.float32), precision=lax.Precision.HIGHEST)

    values = lax.map(one_head, (sorted_queries, w_uv))
    values = jnp.transpose(values, (1, 0, 2))[inverse].astype(jnp.bfloat16).reshape(ROWS, HEADS * VH)
    return jnp.dot(values, w_out, preferred_element_type=jnp.float32).astype(jnp.bfloat16)
```

```python
import jax
import jax.numpy as jnp
from jax import lax
from jax.experimental import pallas as pl
from jax.experimental.pallas import tpu as pltpu
from jax.sharding import Mesh, PartitionSpec as P

ROPE = 64
NOPE = 128
SCALE = (NOPE + ROPE) ** (-0.5)
NZ, NY, NC, NX = 8, 4, 2, 4
ROWS = 64
GROUP = 16
LAT = 512
VH = 128
MASKED = -1e30
VMEM = 56 * 1024 * 1024


def nt_dot(a, b):
    return lax.dot_general(a, b, (((1,), (1,)), ((), ())), preferred_element_type=jnp.float32)


def attend_kernel(
    place_ref, ids_ref, len_ref, q0_ref, q1_ref, q2_ref, q3_ref, own_ref, peer_ref,
    suf_own_ref, suf_peer_ref, uv_ref, out_ref,
    sorted_ref, keys_ref, latent_ref, value_ref, stat_ref, row_ref,
):
    z, y, own_base, peer_base = place_ref[0], place_ref[1], place_ref[2], place_ref[3]
    q_refs = (q0_ref, q1_ref, q2_ref, q3_ref)
    counts = [jnp.int32(0), jnp.int32(ROWS // 2)]
    for j in range(NY):
        for k in range(NZ):
            chip = lax.rem(z + NZ - k, NZ) * NY + lax.rem(y + NY - j, NY)
            for b in range(2):
                row = chip * 2 + b
                second = ids_ref[row] != 0
                spot = jnp.where(second, counts[1], counts[0])
                counts = [
                    counts[0] + jnp.where(second, 0, 1),
                    counts[1] + jnp.where(second, 1, 0),
                ]
                row_ref[spot] = row
                sorted_ref[pl.ds(pl.multiple_of(spot * GROUP, GROUP), GROUP), :] = q_refs[j][
                    k * 2 + b
                ]
    lane = lax.broadcasted_iota(jnp.int32, (64, 256), 1)
    part = lax.broadcasted_iota(jnp.int32, (64, 256), 0) // GROUP
    inside = lax.rem(lane, 64)
    position = jnp.where(inside < 32, own_base + inside, peer_base + inside - 32)
    same = lane // 64 == part
    block = 256
    for t in range(ROWS * GROUP // block):
        k = t // 2
        q = sorted_ref[pl.ds(t * block, block), :]
        s_own = jnp.dot(q, own_ref[k], preferred_element_type=jnp.float32)
        s_peer = jnp.dot(q, peer_ref[k], preferred_element_type=jnp.float32)
        suffix = []
        for g in range(4):
            group = t * 4 + g
            limit = jnp.zeros((64, 256), jnp.int32)
            for i in range(4):
                row = row_ref[group * 4 + i]
                keys_ref[group, pl.ds(i * 64, 32), :] = suf_own_ref[row]
                keys_ref[group, pl.ds(i * 64 + 32, 32), :] = suf_peer_ref[row]
                limit = jnp.where(part == i, len_ref[row], limit)
            s = nt_dot(q[g * 64:(g + 1) * 64], keys_ref[group])
            suffix.append(jnp.where(jnp.logical_and(same, position < limit), s, MASKED))
        s_suf = jnp.concatenate(suffix, axis=0)
        peak = jnp.maximum(
            jnp.maximum(s_own.max(-1, keepdims=True), s_peer.max(-1, keepdims=True)),
            s_suf.max(-1, keepdims=True),
        )
        w_own = jnp.exp((s_own - peak) * SCALE)
        w_peer = jnp.exp((s_peer - peak) * SCALE)
        w_suf = jnp.exp((s_suf - peak) * SCALE)
        total = (
            w_own.sum(-1, keepdims=True)
            + w_peer.sum(-1, keepdims=True)
            + w_suf.sum(-1, keepdims=True)
        )
        acc = nt_dot(w_own.astype(jnp.bfloat16), own_ref[k, :LAT, :])
        acc = acc + nt_dot(w_peer.astype(jnp.bfloat16), peer_ref[k, :LAT, :])
        w_suf = w_suf.astype(jnp.bfloat16)
        acc = acc + jnp.concatenate(
            [
                jnp.dot(
                    w_suf[g * 64:(g + 1) * 64],
                    keys_ref[t * 4 + g, :, :LAT],
                    preferred_element_type=jnp.float32,
                )
                for g in range(4)
            ],
            axis=0,
        )
        acc = acc / total
        for c in range(LAT // 128):
            latent_ref[c, pl.ds(t * block, block), :] = acc[:, c * 128:(c + 1) * 128]
        mass = peak * SCALE + jnp.log(total)
        for i in range(block // GROUP):
            row = row_ref[t * (block // GROUP) + i]
            stat_ref[pl.ds(pl.multiple_of(row * GROUP, GROUP), GROUP), :] = jnp.broadcast_to(
                mass[i * GROUP:(i + 1) * GROUP], (GROUP, 128)
            )
    for h in range(GROUP):
        rows = jnp.concatenate(
            [latent_ref[c, pl.ds(h, ROWS, stride=GROUP), :] for c in range(LAT // 128)], axis=1
        ).astype(jnp.bfloat16)
        value_ref[pl.ds(h, ROWS, stride=GROUP), :] = jnp.dot(
            rows, uv_ref[h], preferred_element_type=jnp.float32
        )
    for i in range(ROWS):
        row = row_ref[i]
        out_ref[row // 2, lax.rem(row, 2)] = value_ref[pl.ds(i * GROUP, GROUP), :].astype(
            jnp.bfloat16
        )
    diagonal = lax.broadcasted_iota(jnp.int32, (128, 128), 0) == lax.broadcasted_iota(
        jnp.int32, (128, 128), 1
    )
    line = lax.broadcasted_iota(jnp.int32, (GROUP, 128), 0)
    for b in range(ROWS * GROUP // 128):
        mass = jnp.where(diagonal, stat_ref[pl.ds(b * 128, 128), :], 0.0).sum(0, keepdims=True)
        high = mass.astype(jnp.bfloat16).astype(jnp.float32)
        middle = (mass - high).astype(jnp.bfloat16).astype(jnp.float32)
        low = mass - high - middle
        stats = jnp.where(
            line == 0, high, jnp.where(line == 1, middle, jnp.where(line == 2, low, 0.0))
        ).astype(jnp.bfloat16)
        for i in range(4):
            out_ref[b * 4 + i, 2] = stats


def attend(place, ids, lens, qs, own, peer, suf_own, suf_peer, uv):
    smem = pl.BlockSpec(memory_space=pltpu.SMEM)
    vmem = pl.BlockSpec(memory_space=pltpu.VMEM)
    return pl.pallas_call(
        attend_kernel,
        out_shape=jax.ShapeDtypeStruct((NZ * NY, 3, GROUP, VH), jnp.bfloat16),
        in_specs=[smem] * 3 + [vmem] * 9,
        out_specs=vmem,
        scratch_shapes=[
            pltpu.VMEM((ROWS * GROUP, LAT + ROPE), jnp.bfloat16),
            pltpu.VMEM((ROWS // 4, 256, LAT + ROPE), jnp.bfloat16),
            pltpu.VMEM((LAT // 128, ROWS * GROUP, 128), jnp.float32),
            pltpu.VMEM((ROWS * GROUP, VH), jnp.float32),
            pltpu.VMEM((ROWS * GROUP, 128), jnp.float32),
            pltpu.SMEM((ROWS,), jnp.int32),
        ],
        compiler_params=pltpu.CompilerParams(vmem_limit_bytes=VMEM),
        cost_estimate=pl.CostEstimate(
            flops=2 * 1024 * 2200 * 1088, bytes_accessed=14 * 2**20, transcendentals=2 * 2**20
        ),
    )(place, ids, lens, *qs, own, peer, suf_own, suf_peer, uv)


def combine_kernel(place_ref, got_ref, out_ref, turned_ref):
    mass = got_ref[:, 2].astype(jnp.float32).sum(1)
    weight = jnp.exp(mass - mass.max(0, keepdims=True))
    weight = weight / weight.sum(0, keepdims=True)
    turned_ref[...] = jnp.concatenate([weight, jnp.zeros((96, 128), jnp.float32)], axis=0).T
    start = pl.multiple_of(lax.rem(place_ref[1], 4) * 32, 32)
    column = turned_ref[pl.ds(start, 32), :]
    total = jnp.zeros((32, VH), jnp.float32)
    for d in range(NZ * NY):
        part = jnp.concatenate([got_ref[d, 0], got_ref[d, 1]], axis=0).astype(jnp.float32)
        total = total + column[:, d:d + 1] * part
    total = total.astype(jnp.bfloat16)
    for d in range(NZ * NY):
        out_ref[d, 0] = total[:GROUP]
        out_ref[d, 1] = total[GROUP:]


def combine(place, got):
    return pl.pallas_call(
        combine_kernel,
        out_shape=jax.ShapeDtypeStruct((NZ * NY, 2, GROUP, VH), jnp.bfloat16),
        in_specs=[pl.BlockSpec(memory_space=pltpu.SMEM), pl.BlockSpec(memory_space=pltpu.VMEM)],
        out_specs=pl.BlockSpec(memory_space=pltpu.VMEM),
        scratch_shapes=[pltpu.VMEM((128, 128), jnp.float32)],
        compiler_params=pltpu.CompilerParams(vmem_limit_bytes=VMEM),
    )(place, got)


def project_kernel(place_ref, values_ref, own_ref, peer_ref, out_ref, wide_ref):
    core = place_ref[4]
    for r in range(ROWS):
        wide_ref[pl.ds(r * GROUP, GROUP), :] = values_ref[r // 2, r % 2].astype(jnp.float32)
    flat = jnp.concatenate(
        [wide_ref[pl.ds(h, ROWS, stride=GROUP), :].astype(jnp.bfloat16) for h in range(GROUP)],
        axis=1,
    )
    mine = nt_dot(own_ref[...], flat)
    other = nt_dot(peer_ref[...], flat)
    for x in range(NX):
        out_ref[core * NX + x] = mine[x * 32:(x + 1) * 32]
        out_ref[(1 - core) * NX + x] = other[x * 32:(x + 1) * 32]


def project(place, values, own, peer):
    vmem = pl.BlockSpec(memory_space=pltpu.VMEM)
    return pl.pallas_call(
        project_kernel,
        out_shape=jax.ShapeDtypeStruct((NC * NX, 32, ROWS), jnp.float32),
        in_specs=[pl.BlockSpec(memory_space=pltpu.SMEM), vmem, vmem, vmem],
        out_specs=vmem,
        scratch_shapes=[pltpu.VMEM((ROWS * GROUP, VH), jnp.float32)],
        compiler_params=pltpu.CompilerParams(vmem_limit_bytes=VMEM),
    )(place, values, own, peer)


def shift(x, axis, size, by):
    return lax.ppermute(x, axis, [(i, (i + by) % size) for i in range(size)])


def per_device(queries, prompt_cache, suffix_cache, prompt_ids, suffix_len, w_uv, w_out):
    z, y, core = lax.axis_index("z"), lax.axis_index("y"), lax.axis_index("c")
    chip = z * NY + y
    own_base = (chip * 2 + core) * 32
    peer_base = (chip * 2 + 1 - core) * 32
    place = jnp.stack([z, y, own_base, peer_base, core]).astype(jnp.int32)
    mine = lax.all_to_all(queries, "c", 1, 0, tiled=True)
    own = jnp.transpose(prompt_cache, (0, 2, 1))
    peer = shift(own, "c", NC, 1)
    suf_peer = shift(suffix_cache, "c", NC, 1)
    w_t = jnp.pad(w_out.T.reshape(NX, 28, -1), ((0, 0), (0, 4), (0, 0))).reshape(NX * 32, -1)
    width = GROUP * VH
    w_own = lax.dynamic_slice_in_dim(w_t, core * width, width, 1)
    w_peer = shift(lax.dynamic_slice_in_dim(w_t, (1 - core) * width, width, 1), "c", NC, 1)
    uv = lax.dynamic_slice_in_dim(w_uv, core * GROUP, GROUP, 0)
    along_z = jnp.concatenate([mine] + [shift(mine, "z", NZ, k) for k in range(1, NZ)], axis=0)
    qs = [along_z] + [shift(along_z, "y", NY, j) for j in range(1, NY)]
    parts = attend(place, prompt_ids, suffix_len, qs, own, peer, suffix_cache, suf_peer, uv)
    got = lax.all_to_all(parts, ("z", "y"), 0, 0, tiled=True)
    values = lax.all_to_all(combine(place, got), ("z", "y"), 0, 0, tiled=True)
    shares = project(place, values, w_own, w_peer)
    summed = lax.all_to_all(shares, ("c", "x"), 0, 0, tiled=True).sum(0)
    return summed[:28].astype(jnp.bfloat16).T


def solution(mesh):
    whole = ("z", "y", "c", "x")
    kv = ("z", "y", "c")
    split = Mesh(mesh.devices.reshape(NZ, NY, NC, NX), whole)
    placed = (
        P(kv, "x", None),
        P(None, kv, None),
        P(None, kv, None),
        P(),
        P(),
        P("x", None, None),
        P("x", kv),
    )
    return jax.shard_map(
        per_device, mesh=split, in_specs=placed, out_specs=P(None, whole), check_vma=False
    )
```

```python
import jax
import jax.numpy as jnp
from jax import lax
from jax.experimental import pallas as pl
from jax.experimental.pallas import tpu as pltpu
from jax.sharding import Mesh, PartitionSpec as P

ROPE = 64
NOPE = 128
SCALE = (NOPE + ROPE) ** (-0.5)
LOG2E = 1.4426950408889634
NZ, NY, NC, NX = 8, 4, 2, 4
CHIPS = NZ * NY
HEADS = 32
LAT = 512
VH = 128
COLUMNS = 28
MASKED = -1e30
TILE = 8
TILES = CHIPS // TILE + 1
SLOTS = TILES * TILE
KEYS = 64
PACKED = HEADS * (LAT + ROPE) // 128
MIB = 1024 * 1024

SMEM = pl.BlockSpec(memory_space=pltpu.SMEM)
BLOCK = pl.BlockSpec(memory_space=pltpu.VMEM)


def call(kernel, out, specs, out_specs, scratch, limit, flops, *args):
    return pl.pallas_call(
        kernel,
        out_shape=out,
        in_specs=specs,
        out_specs=out_specs,
        scratch_shapes=scratch,
        compiler_params=pltpu.CompilerParams(vmem_limit_bytes=limit * MIB),
        cost_estimate=pl.CostEstimate(flops=flops, bytes_accessed=4 * MIB, transcendentals=0),
    )(*args)


def nt_dot(a, b):
    return lax.dot_general(a, b, (((1,), (1,)), ((), ())), preferred_element_type=jnp.float32)


def pack_kernel(q_ref, out_ref):
    q = q_ref[0]
    parts = [q[:, c * 128:(c + 1) * 128] for c in range(LAT // 128)]
    rope = q[:, LAT:]
    parts.append(jnp.concatenate([rope[:HEADS // 2], rope[HEADS // 2:]], axis=1))
    packed = jnp.concatenate(parts, axis=0)
    for d in range(NZ):
        out_ref[d] = packed


def pack(queries):
    return call(
        pack_kernel,
        jax.ShapeDtypeStruct((NZ, PACKED, 128), jnp.bfloat16),
        [BLOCK],
        BLOCK,
        [],
        8,
        2**20,
        queries,
    )


IDS, LENS = 8, 8 + 2 * CHIPS


def prepare_kernel(
    facts_ref, own_in, uv_in, suf_own_ref, suf_peer_ref, table_ref, keys_ref, own_ref, uv_ref, sem
):
    copies = [
        pltpu.make_async_copy(own_in, own_ref, sem.at[0]),
        pltpu.make_async_copy(uv_in, uv_ref, sem.at[1]),
    ]
    for copy in copies:
        copy.start()
    core = facts_ref[2]
    first = jnp.int32(0)
    for t in range(CHIPS):
        first = first + jnp.where(facts_ref[IDS + 2 * t + core] != 0, 0, 1)
    edge = (first + TILE - 1) // TILE
    table_ref[CHIPS + SLOTS] = edge
    table_ref[CHIPS + SLOTS + 1] = edge + (CHIPS - first + TILE - 1) // TILE
    for s in range(SLOTS):
        table_ref[CHIPS + s] = 0
    low, high = jnp.int32(0), edge * TILE
    for t in range(CHIPS):
        second = facts_ref[IDS + 2 * t + core] != 0
        slot = jnp.where(second, high, low)
        low = low + jnp.where(second, 0, 1)
        high = high + jnp.where(second, 1, 0)
        table_ref[t] = slot
        table_ref[CHIPS + slot] = t
    for s in range(SLOTS):
        t = table_ref[CHIPS + s]
        keys_ref[s // 4, pl.ds(s % 4 * KEYS, 32), :] = suf_own_ref[2 * t + core]
        keys_ref[s // 4, pl.ds(s % 4 * KEYS + 32, 32), :] = suf_peer_ref[2 * t + core]
    for copy in copies:
        copy.wait()


def prepare(facts, own, uv, suf_own, suf_peer):
    away = pl.BlockSpec(memory_space=pl.ANY)
    return call(
        prepare_kernel,
        (
            jax.ShapeDtypeStruct((CHIPS + SLOTS + 8,), jnp.int32),
            jax.ShapeDtypeStruct((SLOTS // 4, 4 * KEYS, LAT + ROPE), jnp.bfloat16),
            jax.ShapeDtypeStruct(own.shape, own.dtype),
            jax.ShapeDtypeStruct(uv.shape, uv.dtype),
        ),
        [SMEM, away, away, BLOCK, BLOCK],
        (SMEM, BLOCK, BLOCK, BLOCK),
        [pltpu.SemaphoreType.DMA((2,))],
        20,
        2**28,
        facts, own, uv, suf_own, suf_peer,
    )


def attend_kernel(
    facts_ref, table_ref, q0_ref, q1_ref, q2_ref, q3_ref, own_ref, peer_ref, keys_ref, uv_ref, out_ref,
    q_ref, latent_ref, value_ref, stat_ref,
):
    own_base, peer_base, core, y = facts_ref[0], facts_ref[1], facts_ref[2], facts_ref[4]
    edge, used = table_ref[CHIPS + SLOTS], table_ref[CHIPS + SLOTS + 1]
    for j, ref in enumerate((q0_ref, q1_ref, q2_ref, q3_ref)):
        for z in range(NZ):
            q_ref[table_ref[z * NY + lax.rem(y + NY - j, NY)]] = ref[z]
    pairs = TILE * HEADS
    group = 4 * HEADS
    lane = lax.broadcasted_iota(jnp.int32, (group, 4 * KEYS), 1)
    part = lax.broadcasted_iota(jnp.int32, (group, 4 * KEYS), 0) // HEADS
    inside = lax.rem(lane, KEYS)
    position = jnp.where(inside < 32, own_base + inside, peer_base + inside - 32)
    position = jnp.where(lane // KEYS == part, position, 2**30)

    def query(slot):
        rope = q_ref[slot, LAT // 128 * HEADS:, :]
        parts = [q_ref[slot, c * HEADS:(c + 1) * HEADS, :] for c in range(LAT // 128)]
        parts.append(jnp.concatenate([rope[:, :ROPE], rope[:, ROPE:]], axis=0))
        return jnp.concatenate(parts, axis=1)

    def tile(i):
        k = jnp.where(i >= edge, 1, 0)
        q = jnp.concatenate([query(i * TILE + r) for r in range(TILE)], axis=0)
        s_own = jnp.dot(q, own_ref[k], preferred_element_type=jnp.float32)
        s_peer = jnp.dot(q, peer_ref[k], preferred_element_type=jnp.float32)
        suffix = []
        for g in range(2):
            limit = jnp.zeros((group, 4 * KEYS), jnp.int32)
            for r in range(4):
                t = table_ref[CHIPS + i * TILE + g * 4 + r]
                limit = jnp.where(part == r, facts_ref[LENS + 2 * t + core], limit)
            s = nt_dot(q[g * group:(g + 1) * group], keys_ref[i * 2 + g])
            suffix.append(jnp.where(position < limit, s, MASKED))
        s_suf = jnp.concatenate(suffix, axis=0)
        peak = jnp.maximum(
            jnp.maximum(s_own.max(-1, keepdims=True), s_peer.max(-1, keepdims=True)),
            s_suf.max(-1, keepdims=True),
        )
        w_own = jnp.exp2((s_own - peak) * (SCALE * LOG2E))
        w_peer = jnp.exp2((s_peer - peak) * (SCALE * LOG2E))
        w_suf = jnp.exp2((s_suf - peak) * (SCALE * LOG2E))
        total = (
            w_own.sum(-1, keepdims=True)
            + w_peer.sum(-1, keepdims=True)
            + w_suf.sum(-1, keepdims=True)
        )
        acc = nt_dot(w_own.astype(jnp.bfloat16), own_ref[k, :LAT, :])
        acc = acc + nt_dot(w_peer.astype(jnp.bfloat16), peer_ref[k, :LAT, :])
        w_suf = w_suf.astype(jnp.bfloat16)
        acc = acc + jnp.concatenate(
            [
                jnp.dot(
                    w_suf[g * group:(g + 1) * group],
                    keys_ref[i * 2 + g, :, :LAT],
                    preferred_element_type=jnp.float32,
                )
                for g in range(2)
            ],
            axis=0,
        )
        acc = acc / total
        for c in range(LAT // 128):
            latent_ref[c, pl.ds(i * pairs, pairs), :] = acc[:, c * 128:(c + 1) * 128]
        stat_ref[pl.ds(i * pairs, pairs), :] = jnp.broadcast_to(
            peak * SCALE + jnp.log(total), (pairs, 128)
        )

    for i in range(TILES - 1):
        tile(i)
    pl.when(used == TILES)(lambda: tile(TILES - 1))
    for h in range(0, HEADS, 2):
        rows = jnp.concatenate(
            [
                jnp.concatenate(
                    [latent_ref[c, pl.ds(h + d, SLOTS, stride=HEADS), :] for d in range(2)], axis=0
                )
                for c in range(LAT // 128)
            ],
            axis=1,
        ).astype(jnp.bfloat16)
        both = jnp.concatenate([uv_ref[h], uv_ref[h + 1]], axis=1)
        values = jnp.dot(rows, both, preferred_element_type=jnp.float32)
        value_ref[pl.ds(h, SLOTS, stride=HEADS), :] = values[:SLOTS, :VH]
        value_ref[pl.ds(h + 1, SLOTS, stride=HEADS), :] = values[SLOTS:, VH:]
    diagonal = lax.broadcasted_iota(jnp.int32, (128, 128), 0) == lax.broadcasted_iota(
        jnp.int32, (128, 128), 1
    )
    spots = [pl.multiple_of(table_ref[t] * HEADS, HEADS) for t in range(CHIPS)]
    for b in range(CHIPS // 4):
        picked = jnp.concatenate(
            [stat_ref[pl.ds(spots[b * 4 + i], HEADS), :] for i in range(4)], axis=0
        )
        mass = jnp.where(diagonal, picked, 0.0).sum(0, keepdims=True)
        high = mass.astype(jnp.bfloat16).astype(jnp.float32)
        middle = (mass - high).astype(jnp.bfloat16).astype(jnp.float32)
        stats = jnp.concatenate(
            [high, middle, mass - high - middle, jnp.zeros((5, 128), jnp.float32)], axis=0
        ).astype(jnp.bfloat16)
        for i in range(4):
            out_ref[b * 4 + i, pl.ds(HEADS, 8), :] = stats
    for t in range(CHIPS):
        out_ref[t, pl.ds(0, HEADS), :] = value_ref[pl.ds(spots[t], HEADS), :].astype(jnp.bfloat16)


def attend(facts, table, qs, own, peer, keys, uv):
    pairs = SLOTS * HEADS
    return call(
        attend_kernel,
        jax.ShapeDtypeStruct((CHIPS, HEADS + 8, VH), jnp.bfloat16),
        [SMEM] * 2 + [BLOCK] * 8,
        BLOCK,
        [
            pltpu.VMEM((SLOTS, PACKED, 128), jnp.bfloat16),
            pltpu.VMEM((LAT // 128, pairs, 128), jnp.float32),
            pltpu.VMEM((pairs, VH), jnp.float32),
            pltpu.VMEM((pairs, 128), jnp.float32),
        ],
        30,
        2 * pairs * 2200 * 1088,
        facts, table, *qs, own, peer, keys, uv,
    )


def combine_kernel(facts_ref, got_ref, out_ref, turned_ref):
    start = pl.multiple_of(lax.rem(facts_ref[3], 4) * HEADS, HEADS)
    stats = got_ref[:, HEADS:HEADS + 8, :].astype(jnp.float32)
    mass = stats[:, 0] + stats[:, 1] + stats[:, 2]
    weight = jnp.exp(mass - mass.max(0, keepdims=True))
    weight = weight / weight.sum(0, keepdims=True)
    turned_ref[...] = jnp.concatenate([weight, jnp.zeros((96, 128), jnp.float32)], axis=0).T
    column = turned_ref[pl.ds(start, HEADS), :]
    total = jnp.zeros((HEADS, VH), jnp.float32)
    for d in range(CHIPS):
        total = total + column[:, d:d + 1] * got_ref[d, :HEADS, :].astype(jnp.float32)
    total = total.astype(jnp.bfloat16)
    for d in range(CHIPS):
        out_ref[d] = total


def combine(facts, got):
    return call(
        combine_kernel,
        jax.ShapeDtypeStruct((CHIPS, HEADS, VH), jnp.bfloat16),
        [SMEM, BLOCK],
        BLOCK,
        [pltpu.VMEM((128, 128), jnp.float32)],
        4,
        2**24,
        facts, got,
    )


def project_kernel(facts_ref, values_ref, own_ref, peer_ref, out_ref, wide_ref):
    core = facts_ref[2]
    for t in range(CHIPS):
        wide_ref[pl.ds(t * HEADS, HEADS), :] = values_ref[t].astype(jnp.float32)
    flat = jnp.concatenate(
        [wide_ref[pl.ds(h, CHIPS, stride=HEADS), :].astype(jnp.bfloat16) for h in range(HEADS)],
        axis=1,
    )
    for ref, to in ((own_ref, core), (peer_ref, 1 - core)):
        shares = nt_dot(ref[...], flat)
        for x in range(NX):
            block = jnp.concatenate(
                [shares[x * COLUMNS:(x + 1) * COLUMNS], jnp.zeros((4, CHIPS), jnp.float32)], axis=0
            )
            out_ref[to * NX + x] = jnp.concatenate(
                [block[8 * i:8 * i + 8] for i in range(4)], axis=1
            )


def project(facts, values, own, peer):
    return call(
        project_kernel,
        jax.ShapeDtypeStruct((NC * NX, 8, 128), jnp.float32),
        [SMEM, BLOCK, BLOCK, BLOCK],
        BLOCK,
        [pltpu.VMEM((CHIPS * HEADS, VH), jnp.float32)],
        8,
        2**27,
        facts, values, own, peer,
    )


def finish_kernel(got_ref, out_ref):
    sides = []
    for core in range(NC):
        summed = sum(got_ref[core * NX + x] for x in range(1, NX)) + got_ref[core * NX]
        sides.append(jnp.concatenate([summed[:, 32 * i:32 * i + 32] for i in range(4)], axis=0))
    both = jnp.concatenate(sides, axis=1).astype(jnp.bfloat16)
    lane = lax.broadcasted_iota(jnp.int32, (64, 64), 0)
    row = lax.broadcasted_iota(jnp.int32, (64, 64), 1)
    chosen = (lane == lax.rem(row, 2) * 32 + row // 2).astype(jnp.float32).astype(jnp.bfloat16)
    mixed = jnp.dot(both, chosen, preferred_element_type=jnp.float32).astype(jnp.bfloat16)
    out_ref[...] = mixed[:COLUMNS]


def finish(got):
    return call(
        finish_kernel,
        jax.ShapeDtypeStruct((COLUMNS, 64), jnp.bfloat16),
        [BLOCK],
        BLOCK,
        [],
        4,
        2**20,
        got,
    )


def swap(x):
    return lax.ppermute(x, "c", [(0, 1), (1, 0)])


def per_device(queries, prompt_cache, suffix_cache, prompt_ids, suffix_len, w_uv, w_out):
    core = lax.axis_index("c")
    chip = lax.axis_index("z") * NY + lax.axis_index("y")
    zero = jnp.zeros((), jnp.int32)
    place = [(chip * 2 + core) * 32, (chip * 2 + 1 - core) * 32, core, chip, lax.axis_index("y")]
    facts = jnp.concatenate([jnp.stack(place + [zero] * 3), prompt_ids, suffix_len])
    facts, queries = lax.optimization_barrier((facts, queries))
    own = jnp.transpose(prompt_cache, (0, 2, 1))
    peer, suf_peer = swap(own), swap(suffix_cache)
    along_z = lax.all_to_all(pack(queries), "z", 0, 0, tiled=True)
    along_z, suf_peer = lax.optimization_barrier((along_z, suf_peer))
    qs = [along_z] + [
        lax.ppermute(along_z, "y", [(i, (i + j) % NY) for i in range(NY)]) for j in range(1, NY)
    ]
    table, keys, own, uv = prepare(facts, own, w_uv, suffix_cache, suf_peer)
    parts = attend(facts, table, qs, own, peer, keys, uv)
    parts, w_t = lax.optimization_barrier((parts, w_out.T))
    w_peer = swap(w_t)
    got = lax.all_to_all(parts, ("z", "y"), 0, 0, tiled=True)
    values = lax.all_to_all(combine(facts, got), ("z", "y"), 0, 0, tiled=True)
    shares = project(facts, values, w_t, w_peer)
    return finish(lax.all_to_all(shares, ("c", "x"), 0, 0, tiled=True)).T


def solution(mesh):
    whole = ("z", "y", "c", "x")
    kv = ("z", "y", "c")
    split = Mesh(mesh.devices.reshape(NZ, NY, NC, NX), whole)
    placed = (
        P(kv, "x", None),
        P(None, kv, None),
        P(None, kv, None),
        P(),
        P(),
        P("x", None, None),
        P("x", kv),
    )
    return jax.shard_map(
        per_device, mesh=split, in_specs=placed, out_specs=P(None, whole), check_vma=False
    )
```

```python
import jax
import jax.numpy as jnp
from jax import lax
from jax.experimental import pallas as pl
from jax.experimental.pallas import tpu as pltpu
from jax.sharding import Mesh, PartitionSpec as P

ROPE = 64
NOPE = 128
SCALE = (NOPE + ROPE) ** (-0.5)
LOG2E = 1.4426950408889634
NZ, NY, NC, NX = 8, 4, 2, 4
CHIPS = NZ * NY
HEADS = 32
LAT = 512
VH = 128
COLUMNS = 28
MASKED = -1e30
TILE = 8
SPARE = TILE // 2
USED = CHIPS + SPARE
SLOTS = 40
KEYS = 64
PACKED = HEADS * (LAT + ROPE) // 128
MIB = 1024 * 1024

SMEM = pl.BlockSpec(memory_space=pltpu.SMEM)
BLOCK = pl.BlockSpec(memory_space=pltpu.VMEM)


def call(kernel, out, specs, out_specs, scratch, limit, flops, *args):
    return pl.pallas_call(
        kernel,
        out_shape=out,
        in_specs=specs,
        out_specs=out_specs,
        scratch_shapes=scratch,
        compiler_params=pltpu.CompilerParams(vmem_limit_bytes=limit * MIB),
        cost_estimate=pl.CostEstimate(flops=flops, bytes_accessed=4 * MIB, transcendentals=0),
    )(*args)


def nt_dot(a, b):
    return lax.dot_general(a, b, (((1,), (1,)), ((), ())), preferred_element_type=jnp.float32)


def pack_kernel(q_ref, out_ref):
    q = q_ref[0]
    parts = [q[:, c * 128:(c + 1) * 128] for c in range(LAT // 128)]
    rope = q[:, LAT:]
    parts.append(jnp.concatenate([rope[:HEADS // 2], rope[HEADS // 2:]], axis=1))
    packed = jnp.concatenate(parts, axis=0)
    for d in range(NZ):
        out_ref[d] = packed


def pack(queries):
    return call(
        pack_kernel,
        jax.ShapeDtypeStruct((NZ, PACKED, 128), jnp.bfloat16),
        [BLOCK],
        BLOCK,
        [],
        8,
        2**20,
        queries,
    )


IDS, LENS = 8, 8 + 2 * CHIPS


def prepare_kernel(
    facts_ref, own_in, uv_in, suf_own_ref, suf_peer_ref, table_ref, keys_ref, own_ref, uv_ref, sem
):
    copies = [
        pltpu.make_async_copy(own_in, own_ref, sem.at[0]),
        pltpu.make_async_copy(uv_in, uv_ref, sem.at[1]),
    ]
    for copy in copies:
        copy.start()
    core = facts_ref[2]
    first = jnp.int32(0)
    for t in range(CHIPS):
        first = first + jnp.where(facts_ref[IDS + 2 * t + core] != 0, 0, 1)
    table_ref[CHIPS + SLOTS] = first
    border = first // TILE * TILE
    few = first - border <= SPARE
    for s in range(SLOTS):
        table_ref[CHIPS + s] = 0
    low, high = jnp.int32(0), first
    for t in range(CHIPS):
        second = facts_ref[IDS + 2 * t + core] != 0
        slot = jnp.where(second, high, low)
        moved = jnp.where(
            second,
            jnp.logical_and(jnp.logical_not(few), slot < border + TILE),
            jnp.logical_and(few, slot >= border),
        )
        base = jnp.where(second, first, border)
        slot = jnp.where(moved, CHIPS + slot - base, slot)
        low = low + jnp.where(second, 0, 1)
        high = high + jnp.where(second, 1, 0)
        table_ref[t] = slot
        table_ref[CHIPS + slot] = t
    for s in range(USED):
        t = table_ref[CHIPS + s]
        keys_ref[s // 4, pl.ds(s % 4 * KEYS, 32), :] = suf_own_ref[2 * t + core]
        keys_ref[s // 4, pl.ds(s % 4 * KEYS + 32, 32), :] = suf_peer_ref[2 * t + core]
    for copy in copies:
        copy.wait()


def prepare(facts, own, uv, suf_own, suf_peer):
    away = pl.BlockSpec(memory_space=pl.ANY)
    return call(
        prepare_kernel,
        (
            jax.ShapeDtypeStruct((CHIPS + SLOTS + 8,), jnp.int32),
            jax.ShapeDtypeStruct((USED // 4, 4 * KEYS, LAT + ROPE), jnp.bfloat16),
            jax.ShapeDtypeStruct(own.shape, own.dtype),
            jax.ShapeDtypeStruct(uv.shape, uv.dtype),
        ),
        [SMEM, away, away, BLOCK, BLOCK],
        (SMEM, BLOCK, BLOCK, BLOCK),
        [pltpu.SemaphoreType.DMA((2,))],
        20,
        2**28,
        facts, own, uv, suf_own, suf_peer,
    )


def attend_kernel(
    facts_ref, table_ref, q0_ref, q1_ref, q2_ref, q3_ref, own_ref, peer_ref, keys_ref, uv_ref, out_ref,
    q_ref, latent_ref, value_ref, stat_ref,
):
    own_base, peer_base, core, y = facts_ref[0], facts_ref[1], facts_ref[2], facts_ref[4]
    first = table_ref[CHIPS + SLOTS]
    for j, ref in enumerate((q0_ref, q1_ref, q2_ref, q3_ref)):
        for z in range(NZ):
            q_ref[table_ref[z * NY + lax.rem(y + NY - j, NY)]] = ref[z]
    group = 4 * HEADS
    lane = lax.broadcasted_iota(jnp.int32, (group, 4 * KEYS), 1)
    part = lax.broadcasted_iota(jnp.int32, (group, 4 * KEYS), 0) // HEADS
    inside = lax.rem(lane, KEYS)
    position = jnp.where(inside < 32, own_base + inside, peer_base + inside - 32)
    position = jnp.where(lane // KEYS == part, position, 2**30)

    def query(slot):
        rope = q_ref[slot, LAT // 128 * HEADS:, :]
        parts = [q_ref[slot, c * HEADS:(c + 1) * HEADS, :] for c in range(LAT // 128)]
        parts.append(jnp.concatenate([rope[:, :ROPE], rope[:, ROPE:]], axis=0))
        return jnp.concatenate(parts, axis=1)

    def tile(start, count, k):
        pairs = count * HEADS
        here = pl.ds(start * HEADS, pairs)
        groups = range(start // 4, (start + count) // 4)
        q = jnp.concatenate([query(start + r) for r in range(count)], axis=0)
        s_own = jnp.dot(q, own_ref[k], preferred_element_type=jnp.float32)
        s_peer = jnp.dot(q, peer_ref[k], preferred_element_type=jnp.float32)
        suffix = []
        for g, n in enumerate(groups):
            limit = jnp.zeros((group, 4 * KEYS), jnp.int32)
            for r in range(4):
                t = table_ref[CHIPS + n * 4 + r]
                limit = jnp.where(part == r, facts_ref[LENS + 2 * t + core], limit)
            s = nt_dot(q[g * group:(g + 1) * group], keys_ref[n])
            suffix.append(jnp.where(position < limit, s, MASKED))
        s_suf = jnp.concatenate(suffix, axis=0)
        peak = jnp.maximum(
            jnp.maximum(s_own.max(-1, keepdims=True), s_peer.max(-1, keepdims=True)),
            s_suf.max(-1, keepdims=True),
        )
        w_own = jnp.exp2((s_own - peak) * (SCALE * LOG2E))
        w_peer = jnp.exp2((s_peer - peak) * (SCALE * LOG2E))
        w_suf = jnp.exp2((s_suf - peak) * (SCALE * LOG2E))
        total = (
            w_own.sum(-1, keepdims=True)
            + w_peer.sum(-1, keepdims=True)
            + w_suf.sum(-1, keepdims=True)
        )
        acc = nt_dot(w_own.astype(jnp.bfloat16), own_ref[k, :LAT, :])
        acc = acc + nt_dot(w_peer.astype(jnp.bfloat16), peer_ref[k, :LAT, :])
        w_suf = w_suf.astype(jnp.bfloat16)
        acc = acc + jnp.concatenate(
            [
                jnp.dot(
                    w_suf[g * group:(g + 1) * group],
                    keys_ref[n, :, :LAT],
                    preferred_element_type=jnp.float32,
                )
                for g, n in enumerate(groups)
            ],
            axis=0,
        )
        acc = acc / total
        for c in range(LAT // 128):
            latent_ref[c, here, :] = acc[:, c * 128:(c + 1) * 128]
        stat_ref[here, :] = jnp.broadcast_to(
            peak * SCALE + jnp.log(total), (pairs, 128)
        )

    border = first // TILE * TILE
    tile(CHIPS, SPARE, jnp.where(first - border <= SPARE, 0, 1))
    for i in range(CHIPS // TILE):
        tile(i * TILE, TILE, jnp.where(i * TILE + SPARE >= first, 1, 0))
    for h in range(0, HEADS, 2):
        rows = jnp.concatenate(
            [
                jnp.concatenate(
                    [latent_ref[c, pl.ds(h + d, SLOTS, stride=HEADS), :] for d in range(2)], axis=0
                )
                for c in range(LAT // 128)
            ],
            axis=1,
        ).astype(jnp.bfloat16)
        both = jnp.concatenate([uv_ref[h], uv_ref[h + 1]], axis=1)
        values = jnp.dot(rows, both, preferred_element_type=jnp.float32)
        value_ref[pl.ds(h, SLOTS, stride=HEADS), :] = values[:SLOTS, :VH]
        value_ref[pl.ds(h + 1, SLOTS, stride=HEADS), :] = values[SLOTS:, VH:]
    diagonal = lax.broadcasted_iota(jnp.int32, (128, 128), 0) == lax.broadcasted_iota(
        jnp.int32, (128, 128), 1
    )
    spots = [pl.multiple_of(table_ref[t] * HEADS, HEADS) for t in range(CHIPS)]
    for b in range(CHIPS // 4):
        picked = jnp.concatenate(
            [stat_ref[pl.ds(spots[b * 4 + i], HEADS), :] for i in range(4)], axis=0
        )
        mass = jnp.where(diagonal, picked, 0.0).sum(0, keepdims=True)
        high = mass.astype(jnp.bfloat16).astype(jnp.float32)
        middle = (mass - high).astype(jnp.bfloat16).astype(jnp.float32)
        stats = jnp.concatenate(
            [high, middle, mass - high - middle, jnp.zeros((5, 128), jnp.float32)], axis=0
        ).astype(jnp.bfloat16)
        for i in range(4):
            out_ref[b * 4 + i, pl.ds(HEADS, 8), :] = stats
    for t in range(CHIPS):
        out_ref[t, pl.ds(0, HEADS), :] = value_ref[pl.ds(spots[t], HEADS), :].astype(jnp.bfloat16)


def attend(facts, table, qs, own, peer, keys, uv):
    pairs = SLOTS * HEADS
    return call(
        attend_kernel,
        jax.ShapeDtypeStruct((CHIPS, HEADS + 8, VH), jnp.bfloat16),
        [SMEM] * 2 + [BLOCK] * 8,
        BLOCK,
        [
            pltpu.VMEM((SLOTS, PACKED, 128), jnp.bfloat16),
            pltpu.VMEM((LAT // 128, pairs, 128), jnp.float32),
            pltpu.VMEM((pairs, VH), jnp.float32),
            pltpu.VMEM((pairs, 128), jnp.float32),
        ],
        30,
        2 * pairs * 2200 * 1088,
        facts, table, *qs, own, peer, keys, uv,
    )


def combine_kernel(facts_ref, got_ref, out_ref, turned_ref):
    start = pl.multiple_of(lax.rem(facts_ref[3], 4) * HEADS, HEADS)
    stats = got_ref[:, HEADS:HEADS + 8, :].astype(jnp.float32)
    mass = stats[:, 0] + stats[:, 1] + stats[:, 2]
    weight = jnp.exp(mass - mass.max(0, keepdims=True))
    weight = weight / weight.sum(0, keepdims=True)
    turned_ref[...] = jnp.concatenate([weight, jnp.zeros((96, 128), jnp.float32)], axis=0).T
    column = turned_ref[pl.ds(start, HEADS), :]
    total = jnp.zeros((HEADS, VH), jnp.float32)
    for d in range(CHIPS):
        total = total + column[:, d:d + 1] * got_ref[d, :HEADS, :].astype(jnp.float32)
    total = total.astype(jnp.bfloat16)
    for d in range(CHIPS):
        out_ref[d] = total


def combine(facts, got):
    return call(
        combine_kernel,
        jax.ShapeDtypeStruct((CHIPS, HEADS, VH), jnp.bfloat16),
        [SMEM, BLOCK],
        BLOCK,
        [pltpu.VMEM((128, 128), jnp.float32)],
        4,
        2**24,
        facts, got,
    )


def project_kernel(facts_ref, values_ref, own_ref, peer_ref, out_ref, wide_ref):
    core = facts_ref[2]
    for t in range(CHIPS):
        wide_ref[pl.ds(t * HEADS, HEADS), :] = values_ref[t].astype(jnp.float32)
    flat = jnp.concatenate(
        [wide_ref[pl.ds(h, CHIPS, stride=HEADS), :].astype(jnp.bfloat16) for h in range(HEADS)],
        axis=1,
    )
    for ref, to in ((own_ref, core), (peer_ref, 1 - core)):
        shares = nt_dot(ref[...], flat)
        for x in range(NX):
            block = jnp.concatenate(
                [shares[x * COLUMNS:(x + 1) * COLUMNS], jnp.zeros((4, CHIPS), jnp.float32)], axis=0
            )
            out_ref[to * NX + x] = jnp.concatenate(
                [block[8 * i:8 * i + 8] for i in range(4)], axis=1
            )


def project(facts, values, own, peer):
    return call(
        project_kernel,
        jax.ShapeDtypeStruct((NC * NX, 8, 128), jnp.float32),
        [SMEM, BLOCK, BLOCK, BLOCK],
        BLOCK,
        [pltpu.VMEM((CHIPS * HEADS, VH), jnp.float32)],
        8,
        2**27,
        facts, values, own, peer,
    )


def finish_kernel(got_ref, out_ref):
    sides = []
    for core in range(NC):
        summed = sum(got_ref[core * NX + x] for x in range(1, NX)) + got_ref[core * NX]
        sides.append(jnp.concatenate([summed[:, 32 * i:32 * i + 32] for i in range(4)], axis=0))
    both = jnp.concatenate(sides, axis=1).astype(jnp.bfloat16)
    lane = lax.broadcasted_iota(jnp.int32, (64, 64), 0)
    row = lax.broadcasted_iota(jnp.int32, (64, 64), 1)
    chosen = (lane == lax.rem(row, 2) * 32 + row // 2).astype(jnp.float32).astype(jnp.bfloat16)
    mixed = jnp.dot(both, chosen, preferred_element_type=jnp.float32).astype(jnp.bfloat16)
    out_ref[...] = mixed[:COLUMNS]


def finish(got):
    return call(
        finish_kernel,
        jax.ShapeDtypeStruct((COLUMNS, 64), jnp.bfloat16),
        [BLOCK],
        BLOCK,
        [],
        4,
        2**20,
        got,
    )


def swap(x):
    return lax.ppermute(x, "c", [(0, 1), (1, 0)])


def per_device(queries, prompt_cache, suffix_cache, prompt_ids, suffix_len, w_uv, w_out):
    core = lax.axis_index("c")
    chip = lax.axis_index("z") * NY + lax.axis_index("y")
    zero = jnp.zeros((), jnp.int32)
    place = [(chip * 2 + core) * 32, (chip * 2 + 1 - core) * 32, core, chip, lax.axis_index("y")]
    facts = jnp.concatenate([jnp.stack(place + [zero] * 3), prompt_ids, suffix_len])
    own = jnp.transpose(prompt_cache, (0, 2, 1))
    peer, suf_peer = swap(own), swap(suffix_cache)
    along_z = lax.all_to_all(pack(queries), "z", 0, 0, tiled=True)
    along_z, suf_peer = lax.optimization_barrier((along_z, suf_peer))
    qs = [along_z] + [
        lax.ppermute(along_z, "y", [(i, (i + j) % NY) for i in range(NY)]) for j in range(1, NY)
    ]
    table, keys, own, uv = prepare(facts, own, w_uv, suffix_cache, suf_peer)
    parts = attend(facts, table, qs, own, peer, keys, uv)
    parts, w_t = lax.optimization_barrier((parts, w_out.T))
    w_peer = swap(w_t)
    got = lax.all_to_all(parts, ("z", "y"), 0, 0, tiled=True)
    values = lax.all_to_all(combine(facts, got), ("z", "y"), 0, 0, tiled=True)
    shares = project(facts, values, w_t, w_peer)
    return finish(lax.all_to_all(shares, ("c", "x"), 0, 0, tiled=True)).T


def solution(mesh):
    whole = ("z", "y", "c", "x")
    kv = ("z", "y", "c")
    split = Mesh(mesh.devices.reshape(NZ, NY, NC, NX), whole)
    placed = (
        P(kv, "x", None),
        P(None, kv, None),
        P(None, kv, None),
        P(),
        P(),
        P("x", None, None),
        P("x", kv),
    )
    return jax.shard_map(
        per_device, mesh=split, in_specs=placed, out_specs=P(None, whole), check_vma=False
    )
```

```python
import jax
import jax.numpy as jnp
from jax import lax
from jax.experimental import pallas as pl
from jax.experimental.pallas import tpu as pltpu
from jax.sharding import Mesh, PartitionSpec as P

ROPE = 64
NOPE = 128
SCALE = (NOPE + ROPE) ** (-0.5)
LOG2E = 1.4426950408889634
NZ, NY, NC, NX = 8, 4, 2, 4
CHIPS = NZ * NY
HEADS = 32
LAT = 512
VH = 128
COLUMNS = 28
MASKED = -1e30
TILE = 8
SPARE = TILE // 2
USED = CHIPS + SPARE
SLOTS = 40
KEYS = 64
PACKED = HEADS * (LAT + ROPE) // 128
MIB = 1024 * 1024

SMEM = pl.BlockSpec(memory_space=pltpu.SMEM)
BLOCK = pl.BlockSpec(memory_space=pltpu.VMEM)


def call(kernel, out, specs, out_specs, scratch, limit, flops, *args):
    return pl.pallas_call(
        kernel,
        out_shape=out,
        in_specs=specs,
        out_specs=out_specs,
        scratch_shapes=scratch,
        compiler_params=pltpu.CompilerParams(vmem_limit_bytes=limit * MIB),
        cost_estimate=pl.CostEstimate(flops=flops, bytes_accessed=4 * MIB, transcendentals=0),
    )(*args)


def nt_dot(a, b):
    return lax.dot_general(a, b, (((1,), (1,)), ((), ())), preferred_element_type=jnp.float32)


def pack_kernel(q_ref, out_ref):
    q = q_ref[0]
    parts = [q[:, c * 128:(c + 1) * 128] for c in range(LAT // 128)]
    rope = q[:, LAT:]
    parts.append(jnp.concatenate([rope[:HEADS // 2], rope[HEADS // 2:]], axis=1))
    packed = jnp.concatenate(parts, axis=0)
    for d in range(NZ):
        out_ref[d] = packed


def pack(queries):
    return call(
        pack_kernel,
        jax.ShapeDtypeStruct((NZ, PACKED, 128), jnp.bfloat16),
        [BLOCK],
        BLOCK,
        [],
        8,
        2**20,
        queries,
    )


IDS, LENS = 8, 8 + 2 * CHIPS


def prepare_kernel(
    facts_ref, own_in, peer_in, uv_in, suf_own_ref, suf_peer_ref, table_ref, keys_ref, peer_ref, sem
):
    del own_in, uv_in
    copy = pltpu.make_async_copy(peer_in, peer_ref, sem)
    copy.start()
    core = facts_ref[2]
    first = jnp.int32(0)
    for t in range(CHIPS):
        first = first + jnp.where(facts_ref[IDS + 2 * t + core] != 0, 0, 1)
    table_ref[CHIPS + SLOTS] = first
    border = first // TILE * TILE
    few = first - border <= SPARE
    for s in range(SLOTS):
        table_ref[CHIPS + s] = 0
    low, high = jnp.int32(0), first
    for t in range(CHIPS):
        second = facts_ref[IDS + 2 * t + core] != 0
        slot = jnp.where(second, high, low)
        moved = jnp.where(
            second,
            jnp.logical_and(jnp.logical_not(few), slot < border + TILE),
            jnp.logical_and(few, slot >= border),
        )
        base = jnp.where(second, first, border)
        slot = jnp.where(moved, CHIPS + slot - base, slot)
        low = low + jnp.where(second, 0, 1)
        high = high + jnp.where(second, 1, 0)
        table_ref[t] = slot
        table_ref[CHIPS + slot] = t
    for s in range(USED):
        t = table_ref[CHIPS + s]
        keys_ref[s // 4, pl.ds(s % 4 * KEYS, 32), :] = suf_own_ref[2 * t + core]
        keys_ref[s // 4, pl.ds(s % 4 * KEYS + 32, 32), :] = suf_peer_ref[2 * t + core]
    copy.wait()


def prepare(facts, own, peer, uv, suf_own, suf_peer):
    away = pl.BlockSpec(memory_space=pl.ANY)
    return call(
        prepare_kernel,
        (
            jax.ShapeDtypeStruct((CHIPS + SLOTS + 8,), jnp.int32),
            jax.ShapeDtypeStruct((USED // 4, 4 * KEYS, LAT + ROPE), jnp.bfloat16),
            jax.ShapeDtypeStruct(peer.shape, peer.dtype),
        ),
        [SMEM, away, away, away, BLOCK, BLOCK],
        (SMEM, BLOCK, BLOCK),
        [pltpu.SemaphoreType.DMA],
        20,
        2**28,
        facts, own, peer, uv, suf_own, suf_peer,
    )


def attend_kernel(
    facts_ref, table_ref, q0_ref, q1_ref, q2_ref, q3_ref, own_ref, peer_ref, keys_ref, uv_ref, out_ref,
    q_ref, latent_ref, value_ref, stat_ref,
):
    own_base, peer_base, core, y = facts_ref[0], facts_ref[1], facts_ref[2], facts_ref[4]
    first = table_ref[CHIPS + SLOTS]
    for j, ref in enumerate((q0_ref, q1_ref, q2_ref, q3_ref)):
        for z in range(NZ):
            q_ref[table_ref[z * NY + lax.rem(y + NY - j, NY)]] = ref[z]
    group = 4 * HEADS
    lane = lax.broadcasted_iota(jnp.int32, (group, 4 * KEYS), 1)
    part = lax.broadcasted_iota(jnp.int32, (group, 4 * KEYS), 0) // HEADS
    inside = lax.rem(lane, KEYS)
    position = jnp.where(inside < 32, own_base + inside, peer_base + inside - 32)
    position = jnp.where(lane // KEYS == part, position, 2**30)

    def query(slot):
        rope = q_ref[slot, LAT // 128 * HEADS:, :]
        parts = [q_ref[slot, c * HEADS:(c + 1) * HEADS, :] for c in range(LAT // 128)]
        parts.append(jnp.concatenate([rope[:, :ROPE], rope[:, ROPE:]], axis=0))
        return jnp.concatenate(parts, axis=1)

    def tile(start, count, k):
        pairs = count * HEADS
        here = pl.ds(start * HEADS, pairs)
        groups = range(start // 4, (start + count) // 4)
        q = jnp.concatenate([query(start + r) for r in range(count)], axis=0)
        s_own = jnp.dot(q, own_ref[k], preferred_element_type=jnp.float32)
        s_peer = jnp.dot(q, peer_ref[k], preferred_element_type=jnp.float32)
        suffix = []
        for g, n in enumerate(groups):
            limit = jnp.zeros((group, 4 * KEYS), jnp.int32)
            for r in range(4):
                t = table_ref[CHIPS + n * 4 + r]
                limit = jnp.where(part == r, facts_ref[LENS + 2 * t + core], limit)
            s = nt_dot(q[g * group:(g + 1) * group], keys_ref[n])
            suffix.append(jnp.where(position < limit, s, MASKED))
        s_suf = jnp.concatenate(suffix, axis=0)
        peak = jnp.maximum(
            jnp.maximum(s_own.max(-1, keepdims=True), s_peer.max(-1, keepdims=True)),
            s_suf.max(-1, keepdims=True),
        )
        w_own = jnp.exp2((s_own - peak) * (SCALE * LOG2E))
        w_peer = jnp.exp2((s_peer - peak) * (SCALE * LOG2E))
        w_suf = jnp.exp2((s_suf - peak) * (SCALE * LOG2E))
        total = (
            w_own.sum(-1, keepdims=True)
            + w_peer.sum(-1, keepdims=True)
            + w_suf.sum(-1, keepdims=True)
        )
        acc = nt_dot(w_own.astype(jnp.bfloat16), own_ref[k, :LAT, :])
        acc = acc + nt_dot(w_peer.astype(jnp.bfloat16), peer_ref[k, :LAT, :])
        w_suf = w_suf.astype(jnp.bfloat16)
        acc = acc + jnp.concatenate(
            [
                jnp.dot(
                    w_suf[g * group:(g + 1) * group],
                    keys_ref[n, :, :LAT],
                    preferred_element_type=jnp.float32,
                )
                for g, n in enumerate(groups)
            ],
            axis=0,
        )
        acc = acc / total
        for c in range(LAT // 128):
            latent_ref[c, here, :] = acc[:, c * 128:(c + 1) * 128]
        stat_ref[here, :] = jnp.broadcast_to(
            peak * SCALE + jnp.log(total), (pairs, 128)
        )

    border = first // TILE * TILE
    tile(CHIPS, SPARE, jnp.where(first - border <= SPARE, 0, 1))
    for i in range(CHIPS // TILE):
        tile(i * TILE, TILE, jnp.where(i * TILE + SPARE >= first, 1, 0))
    for h in range(0, HEADS, 2):
        rows = jnp.concatenate(
            [
                jnp.concatenate(
                    [latent_ref[c, pl.ds(h + d, SLOTS, stride=HEADS), :] for d in range(2)], axis=0
                )
                for c in range(LAT // 128)
            ],
            axis=1,
        ).astype(jnp.bfloat16)
        both = jnp.concatenate([uv_ref[h], uv_ref[h + 1]], axis=1)
        values = jnp.dot(rows, both, preferred_element_type=jnp.float32)
        value_ref[pl.ds(h, SLOTS, stride=HEADS), :] = values[:SLOTS, :VH]
        value_ref[pl.ds(h + 1, SLOTS, stride=HEADS), :] = values[SLOTS:, VH:]
    diagonal = lax.broadcasted_iota(jnp.int32, (128, 128), 0) == lax.broadcasted_iota(
        jnp.int32, (128, 128), 1
    )
    spots = [pl.multiple_of(table_ref[t] * HEADS, HEADS) for t in range(CHIPS)]
    for b in range(CHIPS // 4):
        picked = jnp.concatenate(
            [stat_ref[pl.ds(spots[b * 4 + i], HEADS), :] for i in range(4)], axis=0
        )
        mass = jnp.where(diagonal, picked, 0.0).sum(0, keepdims=True)
        high = mass.astype(jnp.bfloat16).astype(jnp.float32)
        middle = (mass - high).astype(jnp.bfloat16).astype(jnp.float32)
        stats = jnp.concatenate(
            [high, middle, mass - high - middle, jnp.zeros((5, 128), jnp.float32)], axis=0
        ).astype(jnp.bfloat16)
        for i in range(4):
            out_ref[b * 4 + i, pl.ds(HEADS, 8), :] = stats
    for t in range(CHIPS):
        out_ref[t, pl.ds(0, HEADS), :] = value_ref[pl.ds(spots[t], HEADS), :].astype(jnp.bfloat16)


def attend(facts, table, qs, own, peer, keys, uv):
    pairs = SLOTS * HEADS
    return call(
        attend_kernel,
        jax.ShapeDtypeStruct((CHIPS, HEADS + 8, VH), jnp.bfloat16),
        [SMEM] * 2 + [BLOCK] * 8,
        BLOCK,
        [
            pltpu.VMEM((SLOTS, PACKED, 128), jnp.bfloat16),
            pltpu.VMEM((LAT // 128, pairs, 128), jnp.float32),
            pltpu.VMEM((pairs, VH), jnp.float32),
            pltpu.VMEM((pairs, 128), jnp.float32),
        ],
        22,
        2 * pairs * 2200 * 1088,
        facts, table, *qs, own, peer, keys, uv,
    )


def combine_kernel(facts_ref, got_ref, out_ref, turned_ref):
    start = pl.multiple_of(lax.rem(facts_ref[3], 4) * HEADS, HEADS)
    stats = got_ref[:, HEADS:HEADS + 8, :].astype(jnp.float32)
    mass = stats[:, 0] + stats[:, 1] + stats[:, 2]
    weight = jnp.exp(mass - mass.max(0, keepdims=True))
    weight = weight / weight.sum(0, keepdims=True)
    turned_ref[...] = jnp.concatenate([weight, jnp.zeros((96, 128), jnp.float32)], axis=0).T
    column = turned_ref[pl.ds(start, HEADS), :]
    total = jnp.zeros((HEADS, VH), jnp.float32)
    for d in range(CHIPS):
        total = total + column[:, d:d + 1] * got_ref[d, :HEADS, :].astype(jnp.float32)
    total = total.astype(jnp.bfloat16)
    for d in range(CHIPS):
        out_ref[d] = total


def combine(facts, got):
    return call(
        combine_kernel,
        jax.ShapeDtypeStruct((CHIPS, HEADS, VH), jnp.bfloat16),
        [SMEM, BLOCK],
        BLOCK,
        [pltpu.VMEM((128, 128), jnp.float32)],
        4,
        2**24,
        facts, got,
    )


def project_kernel(facts_ref, values_ref, own_ref, peer_ref, out_ref, wide_ref):
    core = facts_ref[2]
    for t in range(CHIPS):
        wide_ref[pl.ds(t * HEADS, HEADS), :] = values_ref[t].astype(jnp.float32)
    flat = jnp.concatenate(
        [wide_ref[pl.ds(h, CHIPS, stride=HEADS), :].astype(jnp.bfloat16) for h in range(HEADS)],
        axis=1,
    )
    for ref, to in ((own_ref, core), (peer_ref, 1 - core)):
        shares = nt_dot(ref[...], flat)
        for x in range(NX):
            block = jnp.concatenate(
                [shares[x * COLUMNS:(x + 1) * COLUMNS], jnp.zeros((4, CHIPS), jnp.float32)], axis=0
            )
            out_ref[to * NX + x] = jnp.concatenate(
                [block[8 * i:8 * i + 8] for i in range(4)], axis=1
            )


def project(facts, values, own, peer):
    return call(
        project_kernel,
        jax.ShapeDtypeStruct((NC * NX, 8, 128), jnp.float32),
        [SMEM, BLOCK, BLOCK, BLOCK],
        BLOCK,
        [pltpu.VMEM((CHIPS * HEADS, VH), jnp.float32)],
        8,
        2**27,
        facts, values, own, peer,
    )


def finish_kernel(got_ref, out_ref):
    sides = []
    for core in range(NC):
        summed = sum(got_ref[core * NX + x] for x in range(1, NX)) + got_ref[core * NX]
        sides.append(jnp.concatenate([summed[:, 32 * i:32 * i + 32] for i in range(4)], axis=0))
    both = jnp.concatenate(sides, axis=1).astype(jnp.bfloat16)
    lane = lax.broadcasted_iota(jnp.int32, (64, 64), 0)
    row = lax.broadcasted_iota(jnp.int32, (64, 64), 1)
    chosen = (lane == lax.rem(row, 2) * 32 + row // 2).astype(jnp.float32).astype(jnp.bfloat16)
    mixed = jnp.dot(both, chosen, preferred_element_type=jnp.float32).astype(jnp.bfloat16)
    out_ref[...] = mixed[:COLUMNS]


def finish(got):
    return call(
        finish_kernel,
        jax.ShapeDtypeStruct((COLUMNS, 64), jnp.bfloat16),
        [BLOCK],
        BLOCK,
        [],
        4,
        2**20,
        got,
    )


def swap(x):
    return lax.ppermute(x, "c", [(0, 1), (1, 0)])


def per_device(queries, prompt_cache, suffix_cache, prompt_ids, suffix_len, w_uv, w_out):
    core = lax.axis_index("c")
    chip = lax.axis_index("z") * NY + lax.axis_index("y")
    zero = jnp.zeros((), jnp.int32)
    place = [(chip * 2 + core) * 32, (chip * 2 + 1 - core) * 32, core, chip, lax.axis_index("y")]
    facts = jnp.concatenate([jnp.stack(place + [zero] * 3), prompt_ids, suffix_len])
    own = jnp.transpose(prompt_cache, (0, 2, 1))
    peer, suf_peer = swap(own), swap(suffix_cache)
    along_z = lax.all_to_all(pack(queries), "z", 0, 0, tiled=True)
    along_z, suf_peer = lax.optimization_barrier((along_z, suf_peer))
    qs = [along_z] + [
        lax.ppermute(along_z, "y", [(i, (i + j) % NY) for i in range(NY)]) for j in range(1, NY)
    ]
    table, keys, peer = prepare(facts, own, peer, w_uv, suffix_cache, suf_peer)
    qs, keys, w_t = lax.optimization_barrier((qs, keys, w_out.T))
    parts = attend(facts, table, qs, own, peer, keys, w_uv)
    parts, w_peer = lax.optimization_barrier((parts, swap(w_t)))
    got = lax.all_to_all(parts, ("z", "y"), 0, 0, tiled=True)
    values = lax.all_to_all(combine(facts, got), ("z", "y"), 0, 0, tiled=True)
    shares = project(facts, values, w_t, w_peer)
    return finish(lax.all_to_all(shares, ("c", "x"), 0, 0, tiled=True)).T


def solution(mesh):
    whole = ("z", "y", "c", "x")
    kv = ("z", "y", "c")
    split = Mesh(mesh.devices.reshape(NZ, NY, NC, NX), whole)
    placed = (
        P(kv, "x", None),
        P(None, kv, None),
        P(None, kv, None),
        P(),
        P(),
        P("x", None, None),
        P("x", kv),
    )
    return jax.shard_map(
        per_device, mesh=split, in_specs=placed, out_specs=P(None, whole), check_vma=False
    )
```

```python
import jax
import jax.numpy as jnp
from jax import lax
from jax.experimental import pallas as pl
from jax.experimental.pallas import tpu as pltpu
from jax.sharding import Mesh, PartitionSpec as P

ROPE = 64
NOPE = 128
SCALE = (NOPE + ROPE) ** (-0.5)
LOG2E = 1.4426950408889634
NZ, NY, NC, NX = 8, 4, 2, 4
CHIPS = NZ * NY
HEADS = 32
LAT = 512
VH = 128
COLUMNS = 28
MASKED = -1e30
TILE = 8
SPARE = TILE // 2
USED = CHIPS + SPARE
SLOTS = 40
KEYS = 64
PACKED = HEADS * (LAT + ROPE) // 128
MIB = 1024 * 1024

SMEM = pl.BlockSpec(memory_space=pltpu.SMEM)
BLOCK = pl.BlockSpec(memory_space=pltpu.VMEM)


def call(kernel, out, specs, out_specs, scratch, limit, flops, *args):
    return pl.pallas_call(
        kernel,
        out_shape=out,
        in_specs=specs,
        out_specs=out_specs,
        scratch_shapes=scratch,
        compiler_params=pltpu.CompilerParams(vmem_limit_bytes=limit * MIB),
        cost_estimate=pl.CostEstimate(flops=flops, bytes_accessed=4 * MIB, transcendentals=0),
    )(*args)


def nt_dot(a, b):
    return lax.dot_general(a, b, (((1,), (1,)), ((), ())), preferred_element_type=jnp.float32)


def pack_kernel(q_ref, out_ref):
    q = q_ref[0]
    parts = [q[:, c * 128:(c + 1) * 128] for c in range(LAT // 128)]
    rope = q[:, LAT:]
    parts.append(jnp.concatenate([rope[:HEADS // 2], rope[HEADS // 2:]], axis=1))
    packed = jnp.concatenate(parts, axis=0)
    for d in range(NZ):
        out_ref[d] = packed


def pack(queries):
    return call(
        pack_kernel,
        jax.ShapeDtypeStruct((NZ, PACKED, 128), jnp.bfloat16),
        [BLOCK],
        BLOCK,
        [],
        8,
        2**20,
        queries,
    )


IDS, LENS = 8, 8 + 2 * CHIPS


def prepare_kernel(
    facts_ref, own_in, peer_in, uv_in, suf_own_ref, suf_peer_ref, table_ref, keys_ref, peer_ref, sem
):
    del own_in, uv_in
    copy = pltpu.make_async_copy(peer_in, peer_ref, sem)
    copy.start()
    core = facts_ref[2]
    first = jnp.int32(0)
    for t in range(CHIPS):
        first = first + jnp.where(facts_ref[IDS + 2 * t + core] != 0, 0, 1)
    table_ref[CHIPS + SLOTS] = first
    border = first // TILE * TILE
    few = first - border <= SPARE
    for s in range(SLOTS):
        table_ref[CHIPS + s] = 0
    low, high = jnp.int32(0), first
    for t in range(CHIPS):
        second = facts_ref[IDS + 2 * t + core] != 0
        slot = jnp.where(second, high, low)
        moved = jnp.where(
            second,
            jnp.logical_and(jnp.logical_not(few), slot < border + TILE),
            jnp.logical_and(few, slot >= border),
        )
        base = jnp.where(second, first, border)
        slot = jnp.where(moved, CHIPS + slot - base, slot)
        low = low + jnp.where(second, 0, 1)
        high = high + jnp.where(second, 1, 0)
        table_ref[t] = slot
        table_ref[CHIPS + slot] = t
    for s in range(USED):
        t = table_ref[CHIPS + s]
        keys_ref[s // 4, pl.ds(s % 4 * KEYS, 32), :] = suf_own_ref[2 * t + core]
        keys_ref[s // 4, pl.ds(s % 4 * KEYS + 32, 32), :] = suf_peer_ref[2 * t + core]
    copy.wait()


def prepare(facts, own, peer, uv, suf_own, suf_peer):
    away = pl.BlockSpec(memory_space=pl.ANY)
    return call(
        prepare_kernel,
        (
            jax.ShapeDtypeStruct((CHIPS + SLOTS + 8,), jnp.int32),
            jax.ShapeDtypeStruct((USED // 4, 4 * KEYS, LAT + ROPE), jnp.bfloat16),
            jax.ShapeDtypeStruct(peer.shape, peer.dtype),
        ),
        [SMEM, away, away, away, BLOCK, BLOCK],
        (SMEM, BLOCK, BLOCK),
        [pltpu.SemaphoreType.DMA],
        20,
        2**28,
        facts, own, peer, uv, suf_own, suf_peer,
    )


def attend_kernel(
    facts_ref, table_ref, q0_ref, q1_ref, q2_ref, q3_ref, own_ref, peer_ref, keys_ref, uv_ref, out_ref,
    q_ref, latent_ref, value_ref, stat_ref,
):
    own_base, peer_base, core, y = facts_ref[0], facts_ref[1], facts_ref[2], facts_ref[4]
    first = table_ref[CHIPS + SLOTS]
    for j, ref in enumerate((q0_ref, q1_ref, q2_ref, q3_ref)):
        for z in range(NZ):
            q_ref[table_ref[z * NY + lax.rem(y + NY - j, NY)]] = ref[z]
    group = 4 * HEADS
    lane = lax.broadcasted_iota(jnp.int32, (group, 4 * KEYS), 1)
    part = lax.broadcasted_iota(jnp.int32, (group, 4 * KEYS), 0) // HEADS
    inside = lax.rem(lane, KEYS)
    position = jnp.where(inside < 32, own_base + inside, peer_base + inside - 32)
    position = jnp.where(lane // KEYS == part, position, 2**30)

    def query(slot):
        rope = q_ref[slot, LAT // 128 * HEADS:, :]
        parts = [q_ref[slot, c * HEADS:(c + 1) * HEADS, :] for c in range(LAT // 128)]
        parts.append(jnp.concatenate([rope[:, :ROPE], rope[:, ROPE:]], axis=0))
        return jnp.concatenate(parts, axis=1)

    def tile(start, count, k):
        pairs = count * HEADS
        here = pl.ds(start * HEADS, pairs)
        groups = range(start // 4, (start + count) // 4)
        q = jnp.concatenate([query(start + r) for r in range(count)], axis=0)
        s_own = jnp.dot(q, own_ref[k], preferred_element_type=jnp.float32)
        s_peer = jnp.dot(q, peer_ref[k], preferred_element_type=jnp.float32)
        suffix = []
        for g, n in enumerate(groups):
            limit = jnp.zeros((group, 4 * KEYS), jnp.int32)
            for r in range(4):
                t = table_ref[CHIPS + n * 4 + r]
                limit = jnp.where(part == r, facts_ref[LENS + 2 * t + core], limit)
            s = nt_dot(q[g * group:(g + 1) * group], keys_ref[n])
            suffix.append(jnp.where(position < limit, s, MASKED))
        s_suf = jnp.concatenate(suffix, axis=0)
        peak = jnp.maximum(
            jnp.maximum(s_own.max(-1, keepdims=True), s_peer.max(-1, keepdims=True)),
            s_suf.max(-1, keepdims=True),
        )
        w_own = jnp.exp2((s_own - peak) * (SCALE * LOG2E))
        w_peer = jnp.exp2((s_peer - peak) * (SCALE * LOG2E))
        w_suf = jnp.exp2((s_suf - peak) * (SCALE * LOG2E))
        total = (
            w_own.sum(-1, keepdims=True)
            + w_peer.sum(-1, keepdims=True)
            + w_suf.sum(-1, keepdims=True)
        )
        acc = nt_dot(w_own.astype(jnp.bfloat16), own_ref[k, :LAT, :])
        acc = acc + nt_dot(w_peer.astype(jnp.bfloat16), peer_ref[k, :LAT, :])
        w_suf = w_suf.astype(jnp.bfloat16)
        acc = acc + jnp.concatenate(
            [
                jnp.dot(
                    w_suf[g * group:(g + 1) * group],
                    keys_ref[n, :, :LAT],
                    preferred_element_type=jnp.float32,
                )
                for g, n in enumerate(groups)
            ],
            axis=0,
        )
        acc = acc / total
        for c in range(LAT // 128):
            latent_ref[c, here, :] = acc[:, c * 128:(c + 1) * 128]
        stat_ref[here, :] = jnp.broadcast_to(
            peak * SCALE + jnp.log(total), (pairs, 128)
        )

    border = first // TILE * TILE
    tile(CHIPS, SPARE, jnp.where(first - border <= SPARE, 0, 1))
    for i in range(CHIPS // TILE):
        tile(i * TILE, TILE, jnp.where(i * TILE + SPARE >= first, 1, 0))
    for h in range(0, HEADS, 2):
        rows = jnp.concatenate(
            [
                jnp.concatenate(
                    [latent_ref[c, pl.ds(h + d, SLOTS, stride=HEADS), :] for d in range(2)], axis=0
                )
                for c in range(LAT // 128)
            ],
            axis=1,
        ).astype(jnp.bfloat16)
        both = jnp.concatenate([uv_ref[h], uv_ref[h + 1]], axis=1)
        values = jnp.dot(rows, both, preferred_element_type=jnp.float32)
        value_ref[pl.ds(h, SLOTS, stride=HEADS), :] = values[:SLOTS, :VH]
        value_ref[pl.ds(h + 1, SLOTS, stride=HEADS), :] = values[SLOTS:, VH:]
    diagonal = lax.broadcasted_iota(jnp.int32, (128, 128), 0) == lax.broadcasted_iota(
        jnp.int32, (128, 128), 1
    )
    spots = [pl.multiple_of(table_ref[t] * HEADS, HEADS) for t in range(CHIPS)]
    for b in range(CHIPS // 4):
        picked = jnp.concatenate(
            [stat_ref[pl.ds(spots[b * 4 + i], HEADS), :] for i in range(4)], axis=0
        )
        mass = jnp.where(diagonal, picked, 0.0).sum(0, keepdims=True)
        high = mass.astype(jnp.bfloat16).astype(jnp.float32)
        middle = (mass - high).astype(jnp.bfloat16).astype(jnp.float32)
        stats = jnp.concatenate(
            [high, middle, mass - high - middle, jnp.zeros((5, 128), jnp.float32)], axis=0
        ).astype(jnp.bfloat16)
        for i in range(4):
            out_ref[b * 4 + i, pl.ds(HEADS, 8), :] = stats
    for t in range(CHIPS):
        out_ref[t, pl.ds(0, HEADS), :] = value_ref[pl.ds(spots[t], HEADS), :].astype(jnp.bfloat16)


def attend(facts, table, qs, own, peer, keys, uv):
    pairs = SLOTS * HEADS
    return call(
        attend_kernel,
        jax.ShapeDtypeStruct((CHIPS, HEADS + 8, VH), jnp.bfloat16),
        [SMEM] * 2 + [BLOCK] * 8,
        BLOCK,
        [
            pltpu.VMEM((SLOTS, PACKED, 128), jnp.bfloat16),
            pltpu.VMEM((LAT // 128, pairs, 128), jnp.float32),
            pltpu.VMEM((pairs, VH), jnp.float32),
            pltpu.VMEM((pairs, 128), jnp.float32),
        ],
        22,
        2 * pairs * 2200 * 1088,
        facts, table, *qs, own, peer, keys, uv,
    )


def combine_kernel(facts_ref, got_ref, out_ref, turned_ref):
    start = pl.multiple_of(lax.rem(facts_ref[3], 4) * HEADS, HEADS)
    stats = got_ref[:, HEADS:HEADS + 8, :].astype(jnp.float32)
    mass = stats[:, 0] + stats[:, 1] + stats[:, 2]
    weight = jnp.exp(mass - mass.max(0, keepdims=True))
    weight = weight / weight.sum(0, keepdims=True)
    turned_ref[...] = jnp.concatenate([weight, jnp.zeros((96, 128), jnp.float32)], axis=0).T
    column = turned_ref[pl.ds(start, HEADS), :]
    total = jnp.zeros((HEADS, VH), jnp.float32)
    for d in range(CHIPS):
        total = total + column[:, d:d + 1] * got_ref[d, :HEADS, :].astype(jnp.float32)
    total = total.astype(jnp.bfloat16)
    for d in range(CHIPS):
        out_ref[d] = total


def combine(facts, got):
    return call(
        combine_kernel,
        jax.ShapeDtypeStruct((CHIPS, HEADS, VH), jnp.bfloat16),
        [SMEM, BLOCK],
        BLOCK,
        [pltpu.VMEM((128, 128), jnp.float32)],
        4,
        2**24,
        facts, got,
    )


def project_kernel(facts_ref, values_ref, own_ref, peer_ref, out_ref, wide_ref):
    core = facts_ref[2]
    for t in range(CHIPS):
        wide_ref[pl.ds(t * HEADS, HEADS), :] = values_ref[t].astype(jnp.float32)
    flat = jnp.concatenate(
        [wide_ref[pl.ds(h, CHIPS, stride=HEADS), :].astype(jnp.bfloat16) for h in range(HEADS)],
        axis=1,
    )
    for ref, to in ((own_ref, core), (peer_ref, 1 - core)):
        shares = nt_dot(ref[...], flat)
        for x in range(NX):
            block = jnp.concatenate(
                [shares[x * COLUMNS:(x + 1) * COLUMNS], jnp.zeros((4, CHIPS), jnp.float32)], axis=0
            )
            out_ref[to * NX + x] = jnp.concatenate(
                [block[8 * i:8 * i + 8] for i in range(4)], axis=1
            )


def project(facts, values, own, peer):
    return call(
        project_kernel,
        jax.ShapeDtypeStruct((NC * NX, 8, 128), jnp.float32),
        [SMEM, BLOCK, BLOCK, BLOCK],
        BLOCK,
        [pltpu.VMEM((CHIPS * HEADS, VH), jnp.float32)],
        8,
        2**27,
        facts, values, own, peer,
    )


def finish_kernel(got_ref, out_ref):
    sides = []
    for core in range(NC):
        summed = sum(got_ref[core * NX + x] for x in range(1, NX)) + got_ref[core * NX]
        sides.append(jnp.concatenate([summed[:, 32 * i:32 * i + 32] for i in range(4)], axis=0))
    both = jnp.concatenate(sides, axis=1).astype(jnp.bfloat16)
    lane = lax.broadcasted_iota(jnp.int32, (64, 64), 0)
    row = lax.broadcasted_iota(jnp.int32, (64, 64), 1)
    chosen = (lane == lax.rem(row, 2) * 32 + row // 2).astype(jnp.float32).astype(jnp.bfloat16)
    mixed = jnp.dot(both, chosen, preferred_element_type=jnp.float32).astype(jnp.bfloat16)
    out_ref[...] = mixed[:COLUMNS]


def finish(got):
    return call(
        finish_kernel,
        jax.ShapeDtypeStruct((COLUMNS, 64), jnp.bfloat16),
        [BLOCK],
        BLOCK,
        [],
        4,
        2**20,
        got,
    )


def swap(x):
    return lax.ppermute(x, "c", [(0, 1), (1, 0)])


def per_device(queries, prompt_cache, suffix_cache, prompt_ids, suffix_len, w_uv, w_out):
    core = lax.axis_index("c")
    chip = lax.axis_index("z") * NY + lax.axis_index("y")
    zero = jnp.zeros((), jnp.int32)
    place = [(chip * 2 + core) * 32, (chip * 2 + 1 - core) * 32, core, chip, lax.axis_index("y")]
    facts = jnp.concatenate([jnp.stack(place + [zero] * 3), prompt_ids, suffix_len])
    own = jnp.transpose(prompt_cache, (0, 2, 1))
    peer, suf_peer = swap(own), swap(suffix_cache)
    along_z = lax.all_to_all(pack(queries), "z", 0, 0, tiled=True)
    along_z, suf_peer = lax.optimization_barrier((along_z, suf_peer))
    qs = [along_z] + [
        lax.ppermute(along_z, "y", [(i, (i + j) % NY) for i in range(NY)]) for j in range(1, NY)
    ]
    table, keys, peer = prepare(facts, own, peer, w_uv, suffix_cache, suf_peer)
    qs, keys = lax.optimization_barrier((qs, keys))
    parts = attend(facts, table, qs, own, peer, keys, w_uv)
    got = lax.all_to_all(parts, ("z", "y"), 0, 0, tiled=True)
    mine, w_t = lax.optimization_barrier((combine(facts, got), w_out.T))
    w_peer = swap(w_t)
    values = lax.all_to_all(mine, ("z", "y"), 0, 0, tiled=True)
    shares = project(facts, values, w_t, w_peer)
    return finish(lax.all_to_all(shares, ("c", "x"), 0, 0, tiled=True)).T


def solution(mesh):
    whole = ("z", "y", "c", "x")
    kv = ("z", "y", "c")
    split = Mesh(mesh.devices.reshape(NZ, NY, NC, NX), whole)
    placed = (
        P(kv, "x", None),
        P(None, kv, None),
        P(None, kv, None),
        P(),
        P(),
        P("x", None, None),
        P("x", kv),
    )
    return jax.shard_map(
        per_device, mesh=split, in_specs=placed, out_specs=P(None, whole), check_vma=False
    )
```

```python
import jax
import jax.numpy as jnp
from jax import lax
from jax.experimental import pallas as pl
from jax.experimental.pallas import tpu as pltpu
from jax.sharding import Mesh, PartitionSpec as P

ROPE = 64
NOPE = 128
SCALE = (NOPE + ROPE) ** (-0.5)
LOG2E = 1.4426950408889634
NZ, NY, NC, NX = 8, 4, 2, 4
CHIPS = NZ * NY
HEADS = 32
LAT = 512
VH = 128
COLUMNS = 28
MASKED = -1e30
TILE = 8
SPARE = TILE // 2
USED = CHIPS + SPARE
SLOTS = 40
KEYS = 64
PACKED = HEADS * (LAT + ROPE) // 128
MIB = 1024 * 1024

SMEM = pl.BlockSpec(memory_space=pltpu.SMEM)
BLOCK = pl.BlockSpec(memory_space=pltpu.VMEM)


def call(kernel, out, specs, out_specs, scratch, limit, flops, *args):
    return pl.pallas_call(
        kernel,
        out_shape=out,
        in_specs=specs,
        out_specs=out_specs,
        scratch_shapes=scratch,
        compiler_params=pltpu.CompilerParams(vmem_limit_bytes=limit * MIB),
        cost_estimate=pl.CostEstimate(flops=flops, bytes_accessed=4 * MIB, transcendentals=0),
    )(*args)


def nt_dot(a, b):
    return lax.dot_general(a, b, (((1,), (1,)), ((), ())), preferred_element_type=jnp.float32)


def pack_kernel(q_ref, out_ref):
    q = q_ref[0]
    parts = [q[:, c * 128:(c + 1) * 128] for c in range(LAT // 128)]
    rope = q[:, LAT:]
    parts.append(jnp.concatenate([rope[:HEADS // 2], rope[HEADS // 2:]], axis=1))
    packed = jnp.concatenate(parts, axis=0)
    for d in range(NZ):
        out_ref[d] = packed


def pack(queries):
    return call(
        pack_kernel,
        jax.ShapeDtypeStruct((NZ, PACKED, 128), jnp.bfloat16),
        [BLOCK],
        BLOCK,
        [],
        8,
        2**20,
        queries,
    )


IDS, LENS = 8, 8 + 2 * CHIPS


def prepare_kernel(
    facts_ref, own_in, peer_in, uv_in, suf_own_ref, suf_peer_ref, table_ref, keys_ref, peer_ref, sem
):
    del own_in, uv_in
    copy = pltpu.make_async_copy(peer_in, peer_ref, sem)
    copy.start()
    core = facts_ref[2]
    first = jnp.int32(0)
    for t in range(CHIPS):
        first = first + jnp.where(facts_ref[IDS + 2 * t + core] != 0, 0, 1)
    table_ref[CHIPS + SLOTS] = first
    border = first // TILE * TILE
    few = first - border <= SPARE
    for s in range(SLOTS):
        table_ref[CHIPS + s] = 0
    low, high = jnp.int32(0), first
    for t in range(CHIPS):
        second = facts_ref[IDS + 2 * t + core] != 0
        slot = jnp.where(second, high, low)
        moved = jnp.where(
            second,
            jnp.logical_and(jnp.logical_not(few), slot < border + TILE),
            jnp.logical_and(few, slot >= border),
        )
        base = jnp.where(second, first, border)
        slot = jnp.where(moved, CHIPS + slot - base, slot)
        low = low + jnp.where(second, 0, 1)
        high = high + jnp.where(second, 1, 0)
        table_ref[t] = slot
        table_ref[CHIPS + slot] = t
    for s in range(USED):
        t = table_ref[CHIPS + s]
        keys_ref[s // 4, pl.ds(s % 4 * KEYS, 32), :] = suf_own_ref[2 * t + core]
        keys_ref[s // 4, pl.ds(s % 4 * KEYS + 32, 32), :] = suf_peer_ref[2 * t + core]
    copy.wait()


def prepare(facts, own, peer, uv, suf_own, suf_peer):
    away = pl.BlockSpec(memory_space=pl.ANY)
    return call(
        prepare_kernel,
        (
            jax.ShapeDtypeStruct((CHIPS + SLOTS + 8,), jnp.int32),
            jax.ShapeDtypeStruct((USED // 4, 4 * KEYS, LAT + ROPE), jnp.bfloat16),
            jax.ShapeDtypeStruct(peer.shape, peer.dtype),
        ),
        [SMEM, away, away, away, BLOCK, BLOCK],
        (SMEM, BLOCK, BLOCK),
        [pltpu.SemaphoreType.DMA],
        20,
        2**28,
        facts, own, peer, uv, suf_own, suf_peer,
    )


def attend_kernel(
    facts_ref, table_ref, q0_ref, q1_ref, q2_ref, q3_ref, own_ref, peer_ref, keys_ref, uv_ref, out_ref,
    q_ref, latent_ref, value_ref, stat_ref,
):
    own_base, peer_base, core, y = facts_ref[0], facts_ref[1], facts_ref[2], facts_ref[4]
    first = table_ref[CHIPS + SLOTS]
    for j, ref in enumerate((q0_ref, q1_ref, q2_ref, q3_ref)):
        for z in range(NZ):
            q_ref[table_ref[z * NY + lax.rem(y + NY - j, NY)]] = ref[z]
    group = 4 * HEADS
    lane = lax.broadcasted_iota(jnp.int32, (group, 4 * KEYS), 1)
    part = lax.broadcasted_iota(jnp.int32, (group, 4 * KEYS), 0) // HEADS
    inside = lax.rem(lane, KEYS)
    position = jnp.where(inside < 32, own_base + inside, peer_base + inside - 32)
    position = jnp.where(lane // KEYS == part, position, 2**30)

    def query(slot):
        rope = q_ref[slot, LAT // 128 * HEADS:, :]
        parts = [q_ref[slot, c * HEADS:(c + 1) * HEADS, :] for c in range(LAT // 128)]
        parts.append(jnp.concatenate([rope[:, :ROPE], rope[:, ROPE:]], axis=0))
        return jnp.concatenate(parts, axis=1)

    def tile(start, count, k):
        pairs = count * HEADS
        here = pl.ds(start * HEADS, pairs)
        groups = range(start // 4, (start + count) // 4)
        q = jnp.concatenate([query(start + r) for r in range(count)], axis=0)
        s_own = jnp.dot(q, own_ref[k], preferred_element_type=jnp.float32)
        s_peer = jnp.dot(q, peer_ref[k], preferred_element_type=jnp.float32)
        suffix = []
        for g, n in enumerate(groups):
            limit = jnp.zeros((group, 4 * KEYS), jnp.int32)
            for r in range(4):
                t = table_ref[CHIPS + n * 4 + r]
                limit = jnp.where(part == r, facts_ref[LENS + 2 * t + core], limit)
            s = nt_dot(q[g * group:(g + 1) * group], keys_ref[n])
            suffix.append(jnp.where(position < limit, s, MASKED))
        s_suf = jnp.concatenate(suffix, axis=0)
        peak = jnp.maximum(
            jnp.maximum(s_own.max(-1, keepdims=True), s_peer.max(-1, keepdims=True)),
            s_suf.max(-1, keepdims=True),
        )
        w_own = jnp.exp2((s_own - peak) * (SCALE * LOG2E))
        w_peer = jnp.exp2((s_peer - peak) * (SCALE * LOG2E))
        w_suf = jnp.exp2((s_suf - peak) * (SCALE * LOG2E))
        total = (
            w_own.sum(-1, keepdims=True)
            + w_peer.sum(-1, keepdims=True)
            + w_suf.sum(-1, keepdims=True)
        )
        acc = nt_dot(w_own.astype(jnp.bfloat16), own_ref[k, :LAT, :])
        acc = acc + nt_dot(w_peer.astype(jnp.bfloat16), peer_ref[k, :LAT, :])
        w_suf = w_suf.astype(jnp.bfloat16)
        acc = acc + jnp.concatenate(
            [
                jnp.dot(
                    w_suf[g * group:(g + 1) * group],
                    keys_ref[n, :, :LAT],
                    preferred_element_type=jnp.float32,
                )
                for g, n in enumerate(groups)
            ],
            axis=0,
        )
        acc = acc / total
        for c in range(LAT // 128):
            latent_ref[c, here, :] = acc[:, c * 128:(c + 1) * 128]
        stat_ref[here, :] = jnp.broadcast_to(
            peak * SCALE + jnp.log(total), (pairs, 128)
        )

    border = first // TILE * TILE
    tile(CHIPS, SPARE, jnp.where(first - border <= SPARE, 0, 1))
    for i in range(CHIPS // TILE):
        tile(i * TILE, TILE, jnp.where(i * TILE + SPARE >= first, 1, 0))
    for h in range(0, HEADS, 2):
        rows = jnp.concatenate(
            [
                jnp.concatenate(
                    [latent_ref[c, pl.ds(h + d, SLOTS, stride=HEADS), :] for d in range(2)], axis=0
                )
                for c in range(LAT // 128)
            ],
            axis=1,
        ).astype(jnp.bfloat16)
        both = jnp.concatenate([uv_ref[h], uv_ref[h + 1]], axis=1)
        values = jnp.dot(rows, both, preferred_element_type=jnp.float32)
        value_ref[pl.ds(h, SLOTS, stride=HEADS), :] = values[:SLOTS, :VH]
        value_ref[pl.ds(h + 1, SLOTS, stride=HEADS), :] = values[SLOTS:, VH:]
    diagonal = lax.broadcasted_iota(jnp.int32, (128, 128), 0) == lax.broadcasted_iota(
        jnp.int32, (128, 128), 1
    )
    spots = [pl.multiple_of(table_ref[t] * HEADS, HEADS) for t in range(CHIPS)]
    for b in range(CHIPS // 4):
        picked = jnp.concatenate(
            [stat_ref[pl.ds(spots[b * 4 + i], HEADS), :] for i in range(4)], axis=0
        )
        mass = jnp.where(diagonal, picked, 0.0).sum(0, keepdims=True)
        high = mass.astype(jnp.bfloat16).astype(jnp.float32)
        middle = (mass - high).astype(jnp.bfloat16).astype(jnp.float32)
        stats = jnp.concatenate(
            [high, middle, mass - high - middle, jnp.zeros((5, 128), jnp.float32)], axis=0
        ).astype(jnp.bfloat16)
        for i in range(4):
            out_ref[b * 4 + i, pl.ds(HEADS, 8), :] = stats
    for t in range(CHIPS):
        out_ref[t, pl.ds(0, HEADS), :] = value_ref[pl.ds(spots[t], HEADS), :].astype(jnp.bfloat16)


def attend(facts, table, qs, own, peer, keys, uv):
    pairs = SLOTS * HEADS
    return call(
        attend_kernel,
        jax.ShapeDtypeStruct((CHIPS, HEADS + 8, VH), jnp.bfloat16),
        [SMEM] * 2 + [BLOCK] * 8,
        BLOCK,
        [
            pltpu.VMEM((SLOTS, PACKED, 128), jnp.bfloat16),
            pltpu.VMEM((LAT // 128, pairs, 128), jnp.float32),
            pltpu.VMEM((pairs, VH), jnp.float32),
            pltpu.VMEM((pairs, 128), jnp.float32),
        ],
        22,
        2 * pairs * 2200 * 1088,
        facts, table, *qs, own, peer, keys, uv,
    )


def combine_kernel(facts_ref, got_ref, out_ref, turned_ref):
    start = pl.multiple_of(lax.rem(facts_ref[3], 4) * HEADS, HEADS)
    stats = got_ref[:, HEADS:HEADS + 8, :].astype(jnp.float32)
    mass = stats[:, 0] + stats[:, 1] + stats[:, 2]
    weight = jnp.exp(mass - mass.max(0, keepdims=True))
    weight = weight / weight.sum(0, keepdims=True)
    turned_ref[...] = jnp.concatenate([weight, jnp.zeros((96, 128), jnp.float32)], axis=0).T
    column = turned_ref[pl.ds(start, HEADS), :]
    total = jnp.zeros((HEADS, VH), jnp.float32)
    for d in range(CHIPS):
        total = total + column[:, d:d + 1] * got_ref[d, :HEADS, :].astype(jnp.float32)
    total = total.astype(jnp.bfloat16)
    for d in range(CHIPS):
        out_ref[d] = total


def combine(facts, got):
    return call(
        combine_kernel,
        jax.ShapeDtypeStruct((CHIPS, HEADS, VH), jnp.bfloat16),
        [SMEM, BLOCK],
        BLOCK,
        [pltpu.VMEM((128, 128), jnp.float32)],
        4,
        2**24,
        facts, got,
    )


def project_kernel(facts_ref, values_ref, own_ref, peer_ref, out_ref, wide_ref):
    core = facts_ref[2]
    for t in range(CHIPS):
        wide_ref[pl.ds(t * HEADS, HEADS), :] = values_ref[t].astype(jnp.float32)
    flat = jnp.concatenate(
        [wide_ref[pl.ds(h, CHIPS, stride=HEADS), :].astype(jnp.bfloat16) for h in range(HEADS)],
        axis=1,
    )
    for ref, to in ((own_ref, core), (peer_ref, 1 - core)):
        shares = nt_dot(ref[...], flat)
        for x in range(NX):
            block = jnp.concatenate(
                [shares[x * COLUMNS:(x + 1) * COLUMNS], jnp.zeros((4, CHIPS), jnp.float32)], axis=0
            )
            out_ref[to * NX + x] = jnp.concatenate(
                [block[8 * i:8 * i + 8] for i in range(4)], axis=1
            )


def project(facts, values, own, peer):
    return call(
        project_kernel,
        jax.ShapeDtypeStruct((NC * NX, 8, 128), jnp.float32),
        [SMEM, BLOCK, BLOCK, BLOCK],
        BLOCK,
        [pltpu.VMEM((CHIPS * HEADS, VH), jnp.float32)],
        8,
        2**27,
        facts, values, own, peer,
    )


def finish_kernel(got_ref, out_ref):
    sides = []
    for core in range(NC):
        summed = sum(got_ref[core * NX + x] for x in range(1, NX)) + got_ref[core * NX]
        sides.append(jnp.concatenate([summed[:, 32 * i:32 * i + 32] for i in range(4)], axis=0))
    both = jnp.concatenate(sides, axis=1).astype(jnp.bfloat16)
    lane = lax.broadcasted_iota(jnp.int32, (64, 64), 0)
    row = lax.broadcasted_iota(jnp.int32, (64, 64), 1)
    chosen = (lane == lax.rem(row, 2) * 32 + row // 2).astype(jnp.float32).astype(jnp.bfloat16)
    mixed = jnp.dot(both, chosen, preferred_element_type=jnp.float32).astype(jnp.bfloat16)
    out_ref[...] = mixed[:COLUMNS]


def finish(got):
    return call(
        finish_kernel,
        jax.ShapeDtypeStruct((COLUMNS, 64), jnp.bfloat16),
        [BLOCK],
        BLOCK,
        [],
        4,
        2**20,
        got,
    )


def swap(x):
    return lax.ppermute(x, "c", [(0, 1), (1, 0)])


def per_device(queries, prompt_cache, suffix_cache, prompt_ids, suffix_len, w_uv, w_out):
    core = lax.axis_index("c")
    chip = lax.axis_index("z") * NY + lax.axis_index("y")
    zero = jnp.zeros((), jnp.int32)
    place = [(chip * 2 + core) * 32, (chip * 2 + 1 - core) * 32, core, chip, lax.axis_index("y")]
    facts = jnp.concatenate([jnp.stack(place + [zero] * 3), prompt_ids, suffix_len])
    own = jnp.transpose(prompt_cache, (0, 2, 1))
    peer, suf_peer = swap(own), swap(suffix_cache)
    along_z = lax.all_to_all(pack(queries), "z", 0, 0, tiled=True)
    along_z, suf_peer, w_t = lax.optimization_barrier((along_z, suf_peer, w_out.T))
    qs = [along_z] + [
        lax.ppermute(along_z, "y", [(i, (i + j) % NY) for i in range(NY)]) for j in range(1, NY)
    ]
    table, keys, peer = prepare(facts, own, peer, w_uv, suffix_cache, suf_peer)
    qs, keys, w_peer = lax.optimization_barrier((qs, keys, swap(w_t)))
    parts = attend(facts, table, qs, own, peer, keys, w_uv)
    got = lax.all_to_all(parts, ("z", "y"), 0, 0, tiled=True)
    values = lax.all_to_all(combine(facts, got), ("z", "y"), 0, 0, tiled=True)
    shares = project(facts, values, w_t, w_peer)
    return finish(lax.all_to_all(shares, ("c", "x"), 0, 0, tiled=True)).T


def solution(mesh):
    whole = ("z", "y", "c", "x")
    kv = ("z", "y", "c")
    split = Mesh(mesh.devices.reshape(NZ, NY, NC, NX), whole)
    placed = (
        P(kv, "x", None),
        P(None, kv, None),
        P(None, kv, None),
        P(),
        P(),
        P("x", None, None),
        P("x", kv),
    )
    return jax.shard_map(
        per_device, mesh=split, in_specs=placed, out_specs=P(None, whole), check_vma=False
    )
```

```python
import jax
import jax.numpy as jnp
from jax import lax
from jax.experimental import pallas as pl
from jax.experimental.pallas import tpu as pltpu
from jax.sharding import Mesh, PartitionSpec as P

ROPE = 64
NOPE = 128
SCALE = (NOPE + ROPE) ** (-0.5)
LOG2E = 1.4426950408889634
NZ, NY, NC, NX = 8, 4, 2, 4
CHIPS = NZ * NY
HEADS = 32
LAT = 512
VH = 128
COLUMNS = 28
MASKED = -1e30
TILE = 8
SPARE = TILE // 2
USED = CHIPS + SPARE
SLOTS = 40
KEYS = 64
PACKED = HEADS * (LAT + ROPE) // 128
MIB = 1024 * 1024

SMEM = pl.BlockSpec(memory_space=pltpu.SMEM)
BLOCK = pl.BlockSpec(memory_space=pltpu.VMEM)


def call(kernel, out, specs, out_specs, scratch, limit, flops, *args):
    return pl.pallas_call(
        kernel,
        out_shape=out,
        in_specs=specs,
        out_specs=out_specs,
        scratch_shapes=scratch,
        compiler_params=pltpu.CompilerParams(vmem_limit_bytes=limit * MIB),
        cost_estimate=pl.CostEstimate(flops=flops, bytes_accessed=4 * MIB, transcendentals=0),
    )(*args)


def nt_dot(a, b):
    return lax.dot_general(a, b, (((1,), (1,)), ((), ())), preferred_element_type=jnp.float32)


def pack_kernel(q_ref, out_ref):
    q = q_ref[0]
    parts = [q[:, c * 128:(c + 1) * 128] for c in range(LAT // 128)]
    rope = q[:, LAT:]
    parts.append(jnp.concatenate([rope[:HEADS // 2], rope[HEADS // 2:]], axis=1))
    packed = jnp.concatenate(parts, axis=0)
    for d in range(NZ):
        out_ref[d] = packed


def pack(queries):
    return call(
        pack_kernel,
        jax.ShapeDtypeStruct((NZ, PACKED, 128), jnp.bfloat16),
        [BLOCK],
        BLOCK,
        [],
        8,
        2**20,
        queries,
    )


IDS, LENS = 8, 8 + 2 * CHIPS


def prepare_kernel(
    facts_ref, own_in, peer_in, uv_in, suf_own_ref, suf_peer_ref, table_ref, keys_ref, peer_ref, sem
):
    del own_in, uv_in
    copy = pltpu.make_async_copy(peer_in, peer_ref, sem)
    copy.start()
    core = facts_ref[2]
    first = jnp.int32(0)
    for t in range(CHIPS):
        first = first + jnp.where(facts_ref[IDS + 2 * t + core] != 0, 0, 1)
    table_ref[CHIPS + SLOTS] = first
    border = first // TILE * TILE
    few = first - border <= SPARE
    for s in range(SLOTS):
        table_ref[CHIPS + s] = 0
    low, high = jnp.int32(0), first
    for t in range(CHIPS):
        second = facts_ref[IDS + 2 * t + core] != 0
        slot = jnp.where(second, high, low)
        moved = jnp.where(
            second,
            jnp.logical_and(jnp.logical_not(few), slot < border + TILE),
            jnp.logical_and(few, slot >= border),
        )
        base = jnp.where(second, first, border)
        slot = jnp.where(moved, CHIPS + slot - base, slot)
        low = low + jnp.where(second, 0, 1)
        high = high + jnp.where(second, 1, 0)
        table_ref[t] = slot
        table_ref[CHIPS + slot] = t
    for s in range(USED):
        t = table_ref[CHIPS + s]
        keys_ref[s // 4, pl.ds(s % 4 * KEYS, 32), :] = suf_own_ref[2 * t + core]
        keys_ref[s // 4, pl.ds(s % 4 * KEYS + 32, 32), :] = suf_peer_ref[2 * t + core]
    copy.wait()


def prepare(facts, own, peer, uv, suf_own, suf_peer):
    away = pl.BlockSpec(memory_space=pl.ANY)
    return call(
        prepare_kernel,
        (
            jax.ShapeDtypeStruct((CHIPS + SLOTS + 8,), jnp.int32),
            jax.ShapeDtypeStruct((USED // 4, 4 * KEYS, LAT + ROPE), jnp.bfloat16),
            jax.ShapeDtypeStruct(peer.shape, peer.dtype),
        ),
        [SMEM, away, away, away, BLOCK, BLOCK],
        (SMEM, BLOCK, BLOCK),
        [pltpu.SemaphoreType.DMA],
        20,
        2**28,
        facts, own, peer, uv, suf_own, suf_peer,
    )


def attend_kernel(
    facts_ref, table_ref, q0_ref, q1_ref, q2_ref, q3_ref, own_ref, peer_ref, keys_ref, uv_ref, out_ref,
    q_ref, latent_ref, value_ref, stat_ref,
):
    own_base, peer_base, core, y = facts_ref[0], facts_ref[1], facts_ref[2], facts_ref[4]
    first = table_ref[CHIPS + SLOTS]
    for j, ref in enumerate((q0_ref, q1_ref, q2_ref, q3_ref)):
        for z in range(NZ):
            q_ref[table_ref[z * NY + lax.rem(y + NY - j, NY)]] = ref[z]
    group = 4 * HEADS
    lane = lax.broadcasted_iota(jnp.int32, (group, 4 * KEYS), 1)
    part = lax.broadcasted_iota(jnp.int32, (group, 4 * KEYS), 0) // HEADS
    inside = lax.rem(lane, KEYS)
    position = jnp.where(inside < 32, own_base + inside, peer_base + inside - 32)
    position = jnp.where(lane // KEYS == part, position, 2**30)

    def query(slot):
        rope = q_ref[slot, LAT // 128 * HEADS:, :]
        parts = [q_ref[slot, c * HEADS:(c + 1) * HEADS, :] for c in range(LAT // 128)]
        parts.append(jnp.concatenate([rope[:, :ROPE], rope[:, ROPE:]], axis=0))
        return jnp.concatenate(parts, axis=1)

    def tile(start, count, k):
        pairs = count * HEADS
        here = pl.ds(start * HEADS, pairs)
        groups = range(start // 4, (start + count) // 4)
        q = jnp.concatenate([query(start + r) for r in range(count)], axis=0)
        s_own = jnp.dot(q, own_ref[k], preferred_element_type=jnp.float32)
        s_peer = jnp.dot(q, peer_ref[k], preferred_element_type=jnp.float32)
        suffix = []
        for g, n in enumerate(groups):
            limit = jnp.zeros((group, 4 * KEYS), jnp.int32)
            for r in range(4):
                t = table_ref[CHIPS + n * 4 + r]
                limit = jnp.where(part == r, facts_ref[LENS + 2 * t + core], limit)
            s = nt_dot(q[g * group:(g + 1) * group], keys_ref[n])
            suffix.append(jnp.where(position < limit, s, MASKED))
        s_suf = jnp.concatenate(suffix, axis=0)
        peak = jnp.maximum(
            jnp.maximum(s_own.max(-1, keepdims=True), s_peer.max(-1, keepdims=True)),
            s_suf.max(-1, keepdims=True),
        )
        w_own = jnp.exp2((s_own - peak) * (SCALE * LOG2E))
        w_peer = jnp.exp2((s_peer - peak) * (SCALE * LOG2E))
        w_suf = jnp.exp2((s_suf - peak) * (SCALE * LOG2E))
        total = (
            w_own.sum(-1, keepdims=True)
            + w_peer.sum(-1, keepdims=True)
            + w_suf.sum(-1, keepdims=True)
        )
        acc = nt_dot(w_own.astype(jnp.bfloat16), own_ref[k, :LAT, :])
        acc = acc + nt_dot(w_peer.astype(jnp.bfloat16), peer_ref[k, :LAT, :])
        w_suf = w_suf.astype(jnp.bfloat16)
        acc = acc + jnp.concatenate(
            [
                jnp.dot(
                    w_suf[g * group:(g + 1) * group],
                    keys_ref[n, :, :LAT],
                    preferred_element_type=jnp.float32,
                )
                for g, n in enumerate(groups)
            ],
            axis=0,
        )
        acc = acc / total
        for c in range(LAT // 128):
            latent_ref[c, here, :] = acc[:, c * 128:(c + 1) * 128]
        stat_ref[here, :] = jnp.broadcast_to(
            peak * SCALE + jnp.log(total), (pairs, 128)
        )

    border = first // TILE * TILE
    for i in range(CHIPS // TILE):
        tile(i * TILE, TILE, jnp.where(i * TILE + SPARE >= first, 1, 0))
    tile(CHIPS, SPARE, jnp.where(first - border <= SPARE, 0, 1))
    for h in range(0, HEADS, 2):
        rows = jnp.concatenate(
            [
                jnp.concatenate(
                    [latent_ref[c, pl.ds(h + d, SLOTS, stride=HEADS), :] for d in range(2)], axis=0
                )
                for c in range(LAT // 128)
            ],
            axis=1,
        ).astype(jnp.bfloat16)
        both = jnp.concatenate([uv_ref[h], uv_ref[h + 1]], axis=1)
        values = jnp.dot(rows, both, preferred_element_type=jnp.float32)
        value_ref[pl.ds(h, SLOTS, stride=HEADS), :] = values[:SLOTS, :VH]
        value_ref[pl.ds(h + 1, SLOTS, stride=HEADS), :] = values[SLOTS:, VH:]
    diagonal = lax.broadcasted_iota(jnp.int32, (128, 128), 0) == lax.broadcasted_iota(
        jnp.int32, (128, 128), 1
    )
    spots = [pl.multiple_of(table_ref[t] * HEADS, HEADS) for t in range(CHIPS)]
    for b in range(CHIPS // 4):
        picked = jnp.concatenate(
            [stat_ref[pl.ds(spots[b * 4 + i], HEADS), :] for i in range(4)], axis=0
        )
        mass = jnp.where(diagonal, picked, 0.0).sum(0, keepdims=True)
        high = mass.astype(jnp.bfloat16).astype(jnp.float32)
        middle = (mass - high).astype(jnp.bfloat16).astype(jnp.float32)
        stats = jnp.concatenate(
            [high, middle, mass - high - middle, jnp.zeros((5, 128), jnp.float32)], axis=0
        ).astype(jnp.bfloat16)
        for i in range(4):
            out_ref[b * 4 + i, pl.ds(HEADS, 8), :] = stats
    for t in range(CHIPS):
        out_ref[t, pl.ds(0, HEADS), :] = value_ref[pl.ds(spots[t], HEADS), :].astype(jnp.bfloat16)


def attend(facts, table, qs, own, peer, keys, uv):
    pairs = SLOTS * HEADS
    return call(
        attend_kernel,
        jax.ShapeDtypeStruct((CHIPS, HEADS + 8, VH), jnp.bfloat16),
        [SMEM] * 2 + [BLOCK] * 8,
        BLOCK,
        [
            pltpu.VMEM((SLOTS, PACKED, 128), jnp.bfloat16),
            pltpu.VMEM((LAT // 128, pairs, 128), jnp.float32),
            pltpu.VMEM((pairs, VH), jnp.float32),
            pltpu.VMEM((pairs, 128), jnp.float32),
        ],
        22,
        2 * pairs * 2200 * 1088,
        facts, table, *qs, own, peer, keys, uv,
    )


def combine_kernel(facts_ref, got_ref, out_ref, turned_ref):
    start = pl.multiple_of(lax.rem(facts_ref[3], 4) * HEADS, HEADS)
    stats = got_ref[:, HEADS:HEADS + 8, :].astype(jnp.float32)
    mass = stats[:, 0] + stats[:, 1] + stats[:, 2]
    weight = jnp.exp(mass - mass.max(0, keepdims=True))
    weight = weight / weight.sum(0, keepdims=True)
    turned_ref[...] = jnp.concatenate([weight, jnp.zeros((96, 128), jnp.float32)], axis=0).T
    column = turned_ref[pl.ds(start, HEADS), :]
    total = jnp.zeros((HEADS, VH), jnp.float32)
    for d in range(CHIPS):
        total = total + column[:, d:d + 1] * got_ref[d, :HEADS, :].astype(jnp.float32)
    total = total.astype(jnp.bfloat16)
    for d in range(CHIPS):
        out_ref[d] = total


def combine(facts, got):
    return call(
        combine_kernel,
        jax.ShapeDtypeStruct((CHIPS, HEADS, VH), jnp.bfloat16),
        [SMEM, BLOCK],
        BLOCK,
        [pltpu.VMEM((128, 128), jnp.float32)],
        4,
        2**24,
        facts, got,
    )


def project_kernel(facts_ref, values_ref, own_ref, peer_ref, out_ref, wide_ref):
    core = facts_ref[2]
    for t in range(CHIPS):
        wide_ref[pl.ds(t * HEADS, HEADS), :] = values_ref[t].astype(jnp.float32)
    flat = jnp.concatenate(
        [wide_ref[pl.ds(h, CHIPS, stride=HEADS), :].astype(jnp.bfloat16) for h in range(HEADS)],
        axis=1,
    )
    for ref, to in ((own_ref, core), (peer_ref, 1 - core)):
        shares = nt_dot(ref[...], flat)
        for x in range(NX):
            block = jnp.concatenate(
                [shares[x * COLUMNS:(x + 1) * COLUMNS], jnp.zeros((4, CHIPS), jnp.float32)], axis=0
            )
            out_ref[to * NX + x] = jnp.concatenate(
                [block[8 * i:8 * i + 8] for i in range(4)], axis=1
            )


def project(facts, values, own, peer):
    return call(
        project_kernel,
        jax.ShapeDtypeStruct((NC * NX, 8, 128), jnp.float32),
        [SMEM, BLOCK, BLOCK, BLOCK],
        BLOCK,
        [pltpu.VMEM((CHIPS * HEADS, VH), jnp.float32)],
        8,
        2**27,
        facts, values, own, peer,
    )


def finish_kernel(got_ref, out_ref):
    sides = []
    for core in range(NC):
        summed = sum(got_ref[core * NX + x] for x in range(1, NX)) + got_ref[core * NX]
        sides.append(jnp.concatenate([summed[:, 32 * i:32 * i + 32] for i in range(4)], axis=0))
    both = jnp.concatenate(sides, axis=1).astype(jnp.bfloat16)
    lane = lax.broadcasted_iota(jnp.int32, (64, 64), 0)
    row = lax.broadcasted_iota(jnp.int32, (64, 64), 1)
    chosen = (lane == lax.rem(row, 2) * 32 + row // 2).astype(jnp.float32).astype(jnp.bfloat16)
    mixed = jnp.dot(both, chosen, preferred_element_type=jnp.float32).astype(jnp.bfloat16)
    out_ref[...] = mixed[:COLUMNS]


def finish(got):
    return call(
        finish_kernel,
        jax.ShapeDtypeStruct((COLUMNS, 64), jnp.bfloat16),
        [BLOCK],
        BLOCK,
        [],
        4,
        2**20,
        got,
    )


def swap(x):
    return lax.ppermute(x, "c", [(0, 1), (1, 0)])


def per_device(queries, prompt_cache, suffix_cache, prompt_ids, suffix_len, w_uv, w_out):
    core = lax.axis_index("c")
    chip = lax.axis_index("z") * NY + lax.axis_index("y")
    zero = jnp.zeros((), jnp.int32)
    place = [(chip * 2 + core) * 32, (chip * 2 + 1 - core) * 32, core, chip, lax.axis_index("y")]
    facts = jnp.concatenate([jnp.stack(place + [zero] * 3), prompt_ids, suffix_len])
    own = jnp.transpose(prompt_cache, (0, 2, 1))
    peer, suf_peer = swap(own), swap(suffix_cache)
    along_z = lax.all_to_all(pack(queries), "z", 0, 0, tiled=True)
    along_z, suf_peer = lax.optimization_barrier((along_z, suf_peer))
    qs = [along_z] + [
        lax.ppermute(along_z, "y", [(i, (i + j) % NY) for i in range(NY)]) for j in range(1, NY)
    ]
    table, keys, peer = prepare(facts, own, peer, w_uv, suffix_cache, suf_peer)
    qs, keys, w_t = lax.optimization_barrier((qs, keys, w_out.T))
    parts = attend(facts, table, qs, own, peer, keys, w_uv)
    parts, w_peer = lax.optimization_barrier((parts, swap(w_t)))
    got = lax.all_to_all(parts, ("z", "y"), 0, 0, tiled=True)
    values = lax.all_to_all(combine(facts, got), ("z", "y"), 0, 0, tiled=True)
    shares = project(facts, values, w_t, w_peer)
    return finish(lax.all_to_all(shares, ("c", "x"), 0, 0, tiled=True)).T


def solution(mesh):
    whole = ("z", "y", "c", "x")
    kv = ("z", "y", "c")
    split = Mesh(mesh.devices.reshape(NZ, NY, NC, NX), whole)
    placed = (
        P(kv, "x", None),
        P(None, kv, None),
        P(None, kv, None),
        P(),
        P(),
        P("x", None, None),
        P("x", kv),
    )
    return jax.shard_map(
        per_device, mesh=split, in_specs=placed, out_specs=P(None, whole), check_vma=False
    )
```
